128 devices in a mesh: row: 8 (over z, y_lo), col: 16 (over x, y_hi, core).
Axes of the slice: x: 4, y: 4 (y_hi: 2, y_lo: 2; y = y_hi * 2 + y_lo), z: 4, core: 2. Of those that a mesh axis runs over, the one named last changes fastest.
Arguments:
- atom_feat: bfloat16 [16384, 128], P(('row', 'col')), may hold values from -12 to 12
- atom_token: int32 [16384], P(('row', 'col')), may hold values from 0 to 1535, as said below
- window_start: int32 [512], P(('row', 'col')), may hold values from -64 to 16320, as said below
- token_cond: bfloat16 [1536, 768], P('row'), may hold values from -6 to 6
- token_mask: int32 [1536], replicated, may hold values from 0 to 1, as said below
- pair: bfloat16 [1536, 1536, 128], P('row', 'col'), may hold values from -300 to 300
- enc_in: bfloat16 [4, 128, 128], replicated, may hold values from -2 to 2
- enc_out: bfloat16 [128, 128], replicated, may hold values from -0.5 to 0.5
- pool_weight: bfloat16 [128, 768], replicated, may hold values from -0.5 to 0.5
- tok_in: bfloat16 [2, 4, 768, 768], replicated, may hold values from -0.21875 to 0.21875
- tok_out: bfloat16 [2, 768, 768], replicated, may hold values from -0.21875 to 0.21875
- pair_weight: bfloat16 [2, 128, 16], replicated, may hold values from -0.5 to 0.5
- trans_in: bfloat16 [2, 2, 768, 1536], P(None, None, None, 'col'), may hold values from -0.21875 to 0.21875
- trans_out: bfloat16 [2, 1536, 768], P(None, 'col'), may hold values from -0.15625 to 0.15625
- tok_atom: bfloat16 [768, 128], replicated, may hold values from -0.21875 to 0.21875
- dec_in: bfloat16 [4, 128, 128], replicated, may hold values from -2 to 2
- dec_out: bfloat16 [128, 128], replicated, may hold values from -0.5 to 0.5
- pos_out: bfloat16 [3, 128], replicated, may hold values from -0.5 to 0.5
Outputs:
- position_update: float32 [3, 16384], P(None, ('row', 'col'))
The draws below stay inside these ranges and needn't reach their ends.
Inputs may be any that keep to these rules, and one draw needn't show every extreme that they name: `atom_token`: non-decreasing; every token number 0 to 1535 occurs; for every r, the atoms r * 2048 to (r + 1) * 2048 - 1 belong to the tokens r * 192 to (r + 1) * 192 - 1. window_start[b] lies between 32 b - 64 and 32 b - 32. `token_mask`: ones on a leading run of 768 tokens or more, zeros after, at least one zero.
All inputs are finite; a program needn't handle non-finite values.
Results may differ from the reference program's by a relative error of at most 0.029.
Values may be sent and summed in bfloat16 or wider, within the bound.
A program may use at most 128 MiB of HBM per device.

```python
import math
import jax
import jax.numpy as jnp
from jax import lax

CA = 128
HA = 4
C = 768
H = 16
CZ = 128
FFT = 1536
QB = 32
KW = 128
HALO = 64
BLOCKS = 2
TOK_ROW = 192
TOKENS = 1536
ATOM_ROW = 2048
NATOM = 16384


def sign_vector(key):
    key = jax.random.fold_in(key, 700)
    return (jax.random.randint(key, (CA,), 0, 2) * 2 - 1).astype(jnp.float32)


def lift_terms(key, signs):
    hsize = CA // HA
    size = (300.0 / (CA * math.sqrt(hsize))) ** 0.5
    lift = (jax.random.randint(key, (hsize,), 0, 2) * 2 - 1).astype(jnp.float32) * size
    column = jnp.concatenate([lift, jnp.zeros((CA - hsize,), jnp.float32)])
    outer = (signs * CA ** (-0.5))[:, None] * column[None, :]
    empty = jnp.zeros((CA, CA), jnp.float32)
    return jnp.stack([outer, outer, empty, empty])


def draw_atom_feat(key, part):
    signs = sign_vector(key)
    key = jax.random.fold_in(key, 21)
    base_key, pick_key, spot_key, power_key = jax.random.split(key, 4)
    base = jnp.clip(jax.random.normal(base_key, (NATOM, CA), jnp.float32), -6.0, 6.0)
    nblk = NATOM // QB
    chosen = jax.random.randint(pick_key, (nblk,), 0, 4) == 0
    first = jax.random.randint(spot_key, (nblk,), 0, QB)
    inner = jnp.arange(QB, dtype=jnp.int32)[None, :]
    offset = (inner - first[:, None]) % QB
    spot = (offset == 0) | (offset == 11) | (offset == 21)
    hot = (chosen[:, None] & spot).reshape(NATOM)
    power = 1.5 * 4.0 ** jax.random.uniform(power_key, (NATOM,), jnp.float32)
    lifted = jnp.where(hot, power, 0.0)[:, None] * signs[None, :]
    return (base + lifted).astype(jnp.bfloat16)


def draw_enc_in(key, part):
    signs = sign_vector(key)
    key = jax.random.fold_in(key, 41)
    base_key, lift_key = jax.random.split(key)
    spread = CA ** (-0.5)
    base = jnp.clip(jax.random.normal(base_key, (4, CA, CA), jnp.float32), -6.0, 6.0) * spread
    return (base + lift_terms(lift_key, signs)).astype(jnp.bfloat16)


def draw_dec_in(key, part):
    signs = sign_vector(key)
    key = jax.random.fold_in(key, 42)
    base_key, lift_key = jax.random.split(key)
    spread = CA ** (-0.5)
    base = jnp.clip(jax.random.normal(base_key, (4, CA, CA), jnp.float32), -6.0, 6.0) * spread
    return (base + lift_terms(lift_key, signs)).astype(jnp.bfloat16)


def draw_pair(key, part):
    key = jax.random.fold_in(key, 31)
    base_key, row_key, force_key, near_key, gap_key, power_key, sign_key = jax.random.split(key, 7)
    shape = (TOKENS, TOKENS, CZ)
    base = jnp.clip(jax.random.normal(base_key, shape, jnp.float32), -6.0, 6.0)
    half = TOKENS // 2
    rows = jnp.arange(TOKENS, dtype=jnp.int32)
    forced = jax.random.randint(force_key, (), 0, TOKENS)
    hot = (jax.random.randint(row_key, (TOKENS,), 0, 32) == 0) | (rows == forced)
    near = jax.random.randint(near_key, (TOKENS,), 0, half)
    far = (near + 1 + jax.random.randint(gap_key, (TOKENS,), 0, half - 1)) % half
    power = 150.0 * 2.0 ** jax.random.uniform(power_key, (TOKENS,), jnp.float32)
    signs = (jax.random.randint(sign_key, (TOKENS, CZ), 0, 2) * 2 - 1).astype(jnp.float32)
    cols = rows[None, :]
    lead = hot[:, None] & (cols == near[:, None])
    second = hot[:, None] & (cols == far[:, None])
    factor = jnp.where(lead, 1.0, jnp.where(second, 0.992, 0.0)) * power[:, None]
    planted = factor[:, :, None] * signs[:, None, :]
    return jnp.where((lead | second)[:, :, None], planted, base).astype(jnp.bfloat16)


def draw_atom_token(key, part):
    key = jax.random.fold_in(key, 11)
    nrows = NATOM // ATOM_ROW
    scores = jax.random.randint(key, (nrows, ATOM_ROW), 0, 2 ** 17)
    scores = scores * ATOM_ROW + jnp.arange(ATOM_ROW, dtype=jnp.int32)[None, :]
    scores = scores.at[:, 0].set(-1)
    ranks = jnp.argsort(jnp.argsort(scores, axis=1), axis=1)
    starts = (ranks < TOK_ROW).astype(jnp.int32)
    within = jnp.cumsum(starts, axis=1) - 1
    tokens = within + TOK_ROW * jnp.arange(nrows, dtype=jnp.int32)[:, None]
    return tokens.reshape(NATOM).astype(jnp.int32)


def draw_window_start(key, part):
    key = jax.random.fold_in(key, 12)
    first_key, low_key, high_key = jax.random.split(key, 3)
    nblk = NATOM // QB
    reach = HALO - (KW - QB) // 2
    shifts = jax.random.randint(first_key, (nblk,), -reach, reach + 1)
    low = jax.random.randint(low_key, (), 0, nblk // 2)
    high = jax.random.randint(high_key, (), nblk // 2, nblk)
    shifts = shifts.at[low].set(-reach).at[high].set(reach)
    shifts = shifts.at[0].set(-reach).at[nblk - 1].set(reach)
    return (QB * jnp.arange(nblk, dtype=jnp.int32) - (KW - QB) // 2 + shifts).astype(jnp.int32)


def draw_token_mask(key, part):
    key = jax.random.fold_in(key, 13)
    count = jax.random.randint(key, (), TOKENS // 2, TOKENS)
    return (jnp.arange(TOKENS, dtype=jnp.int32) < count).astype(jnp.int32)


def steps_of(own_key, dims, cuts, least, top_value):
    def one(dim, shards_of):
        steps = jax.random.uniform(jax.random.fold_in(jax.random.fold_in(own_key, 6), dim), (shards_of,), jnp.float32, least / len(cuts), top_value / len(cuts))
        return jnp.repeat(jnp.exp(steps), dims[dim] // shards_of).reshape((-1,) + (1,) * (len(dims) - dim - 1))

    gain = one(*cuts[0])
    for cut in cuts[1:]:
        gain = gain * one(*cut)
    return gain


def scatter_about(rng, dims, scale, most, cuts=(), held_as=jnp.bfloat16):
    result = scale * jax.random.normal(rng, dims, jnp.float32)
    if cuts:
        result = result * steps_of(rng, dims, cuts, -0.22, 0.18)
    return jnp.clip(result, -most, most).astype(held_as)


def setup_inputs(seed: int = 0) -> dict:
    streams_of = jax.random.split(jax.random.key(seed), 19)
    atom_feat = draw_atom_feat(jax.random.fold_in(streams_of[18], 71), 0)
    atom_token = draw_atom_token(jax.random.fold_in(streams_of[18], 71), 0)
    window_start = draw_window_start(jax.random.fold_in(streams_of[18], 71), 0)
    token_cond = scatter_about(streams_of[3], (TOKENS, C), 1.0, 6.0, ((0, 8),))
    token_mask = draw_token_mask(jax.random.fold_in(streams_of[18], 71), 0)
    pair = draw_pair(jax.random.fold_in(streams_of[18], 71), 0)
    enc_in = draw_enc_in(jax.random.fold_in(streams_of[18], 71), 0)
    enc_out = scatter_about(streams_of[7], (CA, CA), CA ** -0.5, 0.5)
    pool_weight = scatter_about(streams_of[8], (CA, C), CA ** -0.5, 0.5)
    tok_in = scatter_about(streams_of[9], (BLOCKS, 4, C, C), C ** -0.5, 0.21875)
    tok_out = scatter_about(streams_of[10], (BLOCKS, C, C), C ** -0.5, 0.21875)
    pair_weight = scatter_about(streams_of[11], (BLOCKS, CZ, H), CZ ** -0.5, 0.5)
    trans_in = scatter_about(streams_of[12], (BLOCKS, 2, C, FFT), C ** -0.5, 0.21875, ((3, 16),))
    trans_out = scatter_about(streams_of[13], (BLOCKS, FFT, C), FFT ** -0.5, 0.15625, ((1, 16),))
    tok_atom = scatter_about(streams_of[14], (C, CA), C ** -0.5, 0.21875)
    dec_in = draw_dec_in(jax.random.fold_in(streams_of[18], 71), 0)
    dec_out = scatter_about(streams_of[16], (CA, CA), CA ** -0.5, 0.5)
    pos_out = scatter_about(streams_of[17], (3, CA), CA ** -0.5, 0.5)
    return {"atom_feat": atom_feat, "atom_token": atom_token, "window_start": window_start, "token_cond": token_cond, "token_mask": token_mask, "pair": pair, "enc_in": enc_in, "enc_out": enc_out, "pool_weight": pool_weight, "tok_in": tok_in, "tok_out": tok_out, "pair_weight": pair_weight, "trans_in": trans_in, "trans_out": trans_out, "tok_atom": tok_atom, "dec_in": dec_in, "dec_out": dec_out, "pos_out": pos_out}


def normed(x):
    x = x.astype(jnp.float32)
    cent = x - lax.optimization_barrier(jnp.mean(x, -1, keepdims=True))
    var = lax.optimization_barrier(jnp.mean(cent * cent, -1, keepdims=True))
    return cent * lax.rsqrt(var + 1e-05)

def atom_layer(x, starts, w_in, w_out):
    width = x.shape[1]
    hsize = width // HA
    xn = normed(x).astype(jnp.bfloat16)
    query = jnp.dot(xn, w_in[0], preferred_element_type=jnp.float32).astype(jnp.bfloat16)
    keys = jnp.dot(xn, w_in[1], preferred_element_type=jnp.float32).astype(jnp.bfloat16)
    vals = jnp.dot(xn, w_in[2], preferred_element_type=jnp.float32).astype(jnp.bfloat16)
    gate = jnp.dot(xn, w_in[3], preferred_element_type=jnp.float32)
    both = jnp.concatenate([keys, vals], 1)
    padded = jnp.pad(both, ((HALO, HALO), (0, 0)))
    nblk = NATOM // QB
    local = (starts + HALO).astype(jnp.int32)
    windows = jax.vmap(lambda s: lax.dynamic_slice_in_dim(padded, s, KW, 0))(local)
    glob = starts[:, None] + jnp.arange(KW, dtype=jnp.int32)[None, :]
    valid = (glob >= 0) & (glob < NATOM)
    qblk = query.reshape(nblk, QB, HA, hsize).astype(jnp.float32)
    kblk = windows[:, :, :width].reshape(nblk, KW, HA, hsize).astype(jnp.float32)
    vblk = windows[:, :, width:].reshape(nblk, KW, HA, hsize).astype(jnp.float32)
    scores = jnp.einsum('bqhd,bkhd->bhqk', qblk, kblk) / jnp.sqrt(jnp.float32(hsize))
    scores = jnp.where(valid[:, None, None, :], scores, -1000000000.0)
    top = lax.optimization_barrier(jnp.max(scores, -1, keepdims=True))
    expd = jnp.exp(scores - top)
    total = lax.optimization_barrier(jnp.sum(expd, -1))
    outs = jnp.einsum('bhqk,bkhd->bqhd', expd.astype(jnp.bfloat16).astype(jnp.float32), vblk)
    outs = outs / jnp.transpose(total, (0, 2, 1))[:, :, :, None]
    outs = outs.reshape(NATOM, width)
    gated = (jax.nn.sigmoid(gate) * outs).astype(jnp.bfloat16)
    return (x.astype(jnp.float32) + jnp.dot(gated, w_out, preferred_element_type=jnp.float32)).astype(jnp.bfloat16)

def token_block(act, pair, key_valid, w_in, w_out, w_pair, t_in, t_out):
    hsize = C // H
    xn = normed(act).astype(jnp.bfloat16)
    query = jnp.dot(xn, w_in[0], preferred_element_type=jnp.float32).astype(jnp.bfloat16)
    keys = jnp.dot(xn, w_in[1], preferred_element_type=jnp.float32).astype(jnp.bfloat16)
    vals = jnp.dot(xn, w_in[2], preferred_element_type=jnp.float32).astype(jnp.bfloat16)
    gate = jnp.dot(xn, w_in[3], preferred_element_type=jnp.float32)
    kh = keys.reshape(TOKENS, H, hsize).astype(jnp.float32)
    vh = vals.reshape(TOKENS, H, hsize).astype(jnp.float32)
    qrows = min(128, TOKENS)
    qblocks = query.reshape(TOKENS // qrows, qrows, H, hsize)
    pblocks = pair.reshape(TOKENS // qrows, qrows, TOKENS, CZ)
    wpair = w_pair.astype(jnp.float32)

    def one_block(args):
        qblk, zblk = args
        bias = jnp.einsum('qkc,ch->hqk', zblk.astype(jnp.float32), wpair)
        scores = jnp.einsum('qhd,khd->hqk', qblk.astype(jnp.float32), kh) / jnp.sqrt(jnp.float32(hsize)) + bias
        scores = jnp.where(key_valid[None, None, :], scores, -1000000000.0)
        top = lax.optimization_barrier(jnp.max(scores, -1, keepdims=True))
        expd = jnp.exp(scores - top)
        total = lax.optimization_barrier(jnp.sum(expd, -1))
        outs = jnp.einsum('hqk,khd->qhd', expd.astype(jnp.bfloat16).astype(jnp.float32), vh)
        outs = outs / jnp.transpose(total)[:, :, None]
        return outs.reshape(qrows, C)
    attn = lax.map(one_block, (qblocks, pblocks)).reshape(TOKENS, C)
    gated = (jax.nn.sigmoid(gate) * attn).astype(jnp.bfloat16)
    act = act + jnp.dot(gated, w_out, preferred_element_type=jnp.float32)
    xn2 = normed(act).astype(jnp.bfloat16)
    swish = jax.nn.silu(jnp.dot(xn2, t_in[0], preferred_element_type=jnp.float32))
    hidden = (swish * jnp.dot(xn2, t_in[1], preferred_element_type=jnp.float32)).astype(jnp.bfloat16)
    return act + jnp.dot(hidden, t_out, preferred_element_type=jnp.float32)

def reference(atom_feat, atom_token, window_start, token_cond, token_mask, pair, enc_in, enc_out, pool_weight, tok_in, tok_out, pair_weight, trans_in, trans_out, tok_atom, dec_in, dec_out, pos_out):
    first = atom_layer(atom_feat, window_start, enc_in, enc_out)
    feats = jax.nn.relu(jnp.dot(first, pool_weight, preferred_element_type=jnp.float32)).astype(jnp.bfloat16)
    sums = jax.ops.segment_sum(feats.astype(jnp.float32), atom_token, TOKENS)
    counts = jax.ops.segment_sum(jnp.ones((NATOM,), jnp.float32), atom_token, TOKENS)
    act = sums / counts[:, None] + token_cond.astype(jnp.float32)
    key_valid = token_mask == 1
    for layer in range(BLOCKS):
        act = token_block(act, pair, key_valid, tok_in[layer], tok_out[layer], pair_weight[layer], trans_in[layer], trans_out[layer])
    proj = jnp.dot(normed(act).astype(jnp.bfloat16), tok_atom, preferred_element_type=jnp.float32).astype(jnp.bfloat16)
    spread = jnp.take(proj, atom_token.astype(jnp.int32), axis=0)
    second = (first.astype(jnp.float32) + spread.astype(jnp.float32)).astype(jnp.bfloat16)
    third = atom_layer(second, window_start, dec_in, dec_out)
    return jnp.dot(pos_out, jnp.transpose(normed(third).astype(jnp.bfloat16)), preferred_element_type=jnp.float32)
```

```python
import math

import jax
import jax.numpy as jnp
from jax import lax
from jax.experimental import pallas as pl
from jax.experimental.pallas import tpu as pltpu
from jax.sharding import PartitionSpec as P

MESH = pl.DeviceIdType.MESH
F32 = jnp.float32
BF16 = jnp.bfloat16
NEG = -1000000000.0
NR = 8
NC = 16
NCH = 8
OWN = 6
QT = 96


def dot(a, b):
    return jnp.dot(a, b, preferred_element_type=F32)


def dot_t(a, b):
    return lax.dot_general(a, b, (((1,), (1,)), ((), ())), preferred_element_type=F32)


def normed(x):
    cent = x - jnp.mean(x, -1, keepdims=True)
    var = jnp.mean(cent * cent, -1, keepdims=True)
    return cent * lax.rsqrt(var + 1e-05)


def iota(shape, dim):
    return lax.broadcasted_iota(jnp.int32, shape, dim)


def atom_layer(xf, valid, w_in, w_out):
    n = normed(xf).astype(BF16)
    own = n[:128]
    q = dot(own, w_in[0]).astype(BF16).astype(F32)
    keys = dot(n, w_in[1]).astype(BF16)
    vals = dot(n, w_in[2]).astype(BF16)
    gate = dot(own, w_in[3])
    head = iota((128, 128), 1) // 32
    outs = jnp.zeros((128, 128), F32)
    for h in range(4):
        qh = jnp.where(head == h, q, 0.0).astype(BF16)
        s = dot_t(qh, keys) * (1.0 / math.sqrt(32.0))
        s = jnp.where(valid, s, NEG)
        e = jnp.exp(s - jnp.max(s, -1, keepdims=True))
        total = jnp.sum(e, -1, keepdims=True)
        o = dot(e.astype(BF16), vals) / total
        outs = jnp.where(head == h, o, outs)
    gated = (jax.nn.sigmoid(gate) * outs).astype(BF16)
    return (xf[:128] + dot(gated, w_out[...])).astype(BF16)


def kernel(
    ws,
    tok,
    mask,
    x_in,
    wt,
    cond_h,
    pair_h,
    enc_in_h,
    enc_out_h,
    pool_h,
    tok_in_h,
    tok_out_h,
    tin_h,
    tout_h,
    tok_atom_h,
    dec_in_h,
    dec_out_h,
    pos_h,
    out,
    cond,
    pair,
    enc_in,
    enc_out,
    pool,
    slab,
    wq,
    topad,
    tin,
    tout,
    tok_atom,
    dec_in,
    dec_out,
    pos,
    xh,
    x1all,
    xe,
    zb,
    bb,
    kv,
    ssc,
    ob,
    prt,
    rsb,
    db,
    act,
    acc,
    proj,
    lsem,
    h_ss,
    h_rs,
    x_ss,
    x_rs,
    e_ss,
    e_rs,
    t_ss,
    t_rs,
    b_ss,
    b_rs,
    kv_ss,
    kv_rs,
    o_ss,
    o_rs,
    r_ss,
    r_rs,
    d_ss,
    d_rs,
    p_ss,
    p_rs,
):
    r = lax.axis_index("row")
    c = lax.axis_index("col")
    i = c // 2
    k = c % 2
    sib = (r, c + 1 - 2 * k)
    flat = r * NC + c
    nxt = (flat + 1) % (NR * NC)
    prv = (flat + NR * NC - 1) % (NR * NC)
    nxt = (nxt // NC, nxt % NC)
    prv = (prv // NC, prv % NC)
    is_owner = i < OWN
    is_tail = jnp.logical_and(k == 1, jnp.logical_and(i >= 2, i < OWN))
    is_head = jnp.logical_and(k == 0, i < 4)

    def chip(j):
        return (r, 2 * ((i + j) % NCH) + k)

    def rcopy(src, dst, ss, rs, dev):
        return pltpu.make_async_remote_copy(
            src_ref=src, dst_ref=dst, send_sem=ss, recv_sem=rs, device_id=dev, device_id_type=MESH
        )

    nload = [0]

    def load(src, dst):
        cp = pltpu.make_async_copy(src, dst, lsem.at[nload[0]])
        nload[0] += 1
        cp.start()
        return cp

    ld_pair = [load(pair_h.at[48 * j : 48 * j + 48], pair.at[48 * j : 48 * j + 48]) for j in range(4)]
    ld_enc = [load(enc_in_h, enc_in), load(enc_out_h, enc_out)]
    ld_pool = [
        load(pool_h, pool),
        load(cond_h.at[pl.ds(pl.multiple_of(QT * k, 32), QT)], cond),
    ]
    base = jnp.minimum(128 * ((QT * i) // 128), 512)
    base = pl.multiple_of(base, 128)
    shift = QT * i - base
    ld_slab = [load(tok_in_h.at[:, :, pl.ds(base, 256)], slab)]
    ld_tok = [
        load(tok_out_h, topad.at[:, 0:QT]),
        load(tin_h, tin.at[k]),
        load(tout_h, tout.at[k]),
        load(tok_atom_h, tok_atom),
        load(dec_in_h, dec_in),
        load(dec_out_h, dec_out),
        load(pos_h, pos),
    ]

    topad[:, QT:, :] = jnp.zeros((16, 32, 768), BF16)
    kv[:, :, :, QT:, :] = jnp.zeros((2, 16, 2, 32, 128), BF16)
    proj[...] = jnp.zeros((384, 128), BF16)

    bar = pltpu.get_barrier_semaphore()

    def greet(dev):
        pl.semaphore_signal(bar, inc=1, device_id=dev, device_id_type=MESH)

    for j in range(1, NC):
        greet((r, (c + j) % NC))
    for j in range(1, NR):
        greet(((r + j) % NR, c))
    greet(nxt)
    greet(prv)

    @pl.when(c == 0)
    def _():
        for o in (5, 7, 9, 11):
            greet(((r + NR - 1) % NR, o))

    @pl.when(c == NC - 1)
    def _():
        for o in (0, 2, 4, 6):
            greet(((r + 1) % NR, o))

    extra = jnp.where(jnp.logical_or(is_tail, is_head), 1, 0)
    pl.semaphore_wait(bar, 24 + extra)

    halo = [
        rcopy(x_in.at[64:128], xh.at[1], h_ss.at[0], h_rs.at[1], nxt),
        rcopy(x_in.at[0:64], xh.at[0], h_ss.at[1], h_rs.at[0], prv),
    ]
    for cp in halo:
        cp.start()
    swap = [
        rcopy(tin_h, tin.at[k], t_ss.at[0], t_rs.at[0], sib),
        rcopy(tout_h, tout.at[k], t_ss.at[1], t_rs.at[1], sib),
    ]
    for cp in swap:
        cp.start()

    def bias_half(kp):
        w = wt[...]
        for kb in range(3):

            @pl.loop(0, 12)
            def _(u):
                t = 24 * kb + 2 * u
                rows = []
                for d in range(2):
                    rows.append(pair[QT * kp + t + d])
                    rows.append(pair[QT * kp + 72 + 2 * u + d, 32 * kb : 32 * kb + 32, :])
                res = dot_t(w, jnp.concatenate(rows, 0))
                zf = zb.reshape(32 * 144, 128)
                for d in range(2):
                    for g in range(4):
                        zf[pl.ds(g * 8 * 144 + kp * 72 + t + d, 8, stride=144), :] = res[
                            8 * g : 8 * g + 8, 128 * d : 128 * d + 128
                        ]

    def bias_src(b, dev):
        return zb.at[
            pl.ds(16 * b + 2 * (dev // 2), 2), pl.ds(pl.multiple_of(72 * (dev % 2), 8), 72), :
        ]

    def bias_send(b, j):
        dev = (c + j) % NC
        return rcopy(bias_src(b, dev), bb.at[b, c], b_ss.at[b, j], b_rs.at[b, c], (r, dev))

    ld_pair[0].wait()
    ld_pair[1].wait()
    bias_half(0)

    for cp in ld_enc:
        cp.wait()
    for cp in halo:
        cp.wait_recv()
    rowi = iota((128, 256), 0)
    coli = iota((128, 256), 1)
    glob = flat * 128 + jnp.where(coli < 192, coli, coli - 256)
    start = jnp.where(
        rowi < 64, jnp.where(rowi < 32, ws[0], ws[1]), jnp.where(rowi < 96, ws[2], ws[3])
    )
    start = jnp.maximum(start, 0)
    stop = jnp.where(
        rowi < 64, jnp.where(rowi < 32, ws[0], ws[1]), jnp.where(rowi < 96, ws[2], ws[3])
    ) + 128
    stop = jnp.minimum(stop, NR * NC * 128)
    valid = jnp.logical_and(glob >= start, glob < stop)
    xf = jnp.concatenate([x_in[...], xh[0], xh[1]], 0).astype(F32)
    x1 = atom_layer(xf, valid, enc_in, enc_out)
    tokrow = (tok[...] - 192 * r).astype(F32)
    tokrows = jnp.broadcast_to(tokrow, (16, 128)).astype(BF16)
    x1all[c, 0:16, :] = tokrows
    x1all[c, 16:144, :] = x1
    x1all[c, 144:160, :] = tokrows

    edge = [
        rcopy(x1all.at[c, 80:160], xe.at[1], e_ss.at[0], e_rs.at[1], nxt),
        rcopy(x1all.at[c, 0:80], xe.at[0], e_ss.at[1], e_rs.at[0], prv),
    ]

    def x1_slot(s):
        return x1all.at[s, 0:144]

    x_send = [
        rcopy(x1_slot(c), x1_slot(c), x_ss.at[j], x_rs.at[c], chip(j)) for j in range(1, NCH)
    ]
    x_fwd = []
    for j in range(NCH):
        s = 2 * ((i + j) % NCH) + k
        x_fwd.append(rcopy(x1_slot(s), x1_slot(s), x_ss.at[NCH + j], x_rs.at[s], sib))
    x_far = []
    for j in range(NCH):
        s = 2 * ((i + j) % NCH) + 1 - k
        x_far.append(rcopy(x1_slot(s), x1_slot(s), x_ss.at[NCH + j], x_rs.at[s], sib))
    for cp in x_send:
        cp.start()
    x_fwd[0].start()
    for cp in edge:
        cp.start()

    ld_pair[2].wait()
    ld_pair[3].wait()
    bias_half(1)
    b_send = [[bias_send(b, j) for j in range(1, NC)] for b in range(2)]
    b_own = []
    for b in range(2):
        cp = pltpu.make_async_copy(bias_src(b, c), bb.at[b, c], lsem.at[nload[0] + b])
        cp.start()
        b_own.append(cp)
    for cp in b_send[0]:
        cp.start()

    for cp in ld_slab:
        cp.wait()
    pick = jnp.logical_and(
        iota((256, 128), 0) == iota((256, 128), 1) + shift, iota((256, 128), 1) < QT
    )
    pick = jnp.where(pick, 1.0, 0.0).astype(BF16)

    @pl.loop(0, 8)
    def _(m):
        wq[m] = dot(slab[m], pick).astype(BF16)

    for j in range(1, NCH):
        s = 2 * ((i + j) % NCH) + k
        rcopy(x1_slot(s), x1_slot(s), x_ss.at[0], x_rs.at[s], sib).wait_recv()
        x_fwd[j].start()
    for cp in x_far:
        cp.wait_recv()
    for cp in ld_pool:
        cp.wait()
    acc[...] = jnp.zeros((QT, 768), F32)

    def pool_step(s2, cnt):
        both = jnp.concatenate([x1all[2 * s2, 16:144, :], x1all[2 * s2 + 1, 16:144, :]], 0)
        feats = jnp.maximum(dot(both, pool[...]), 0.0).astype(BF16)
        hots = []
        want = (iota((QT, 128), 0) + QT * k).astype(F32)
        for d in range(2):
            t = x1all[2 * s2 + d, 0:16, :].astype(F32)[0:1]
            hots.append(jnp.where(t == want, 1.0, 0.0))
        acc[...] += dot(jnp.concatenate(hots, 1).astype(BF16), feats)
        return cnt + hots[0] + hots[1]

    cnt = lax.fori_loop(0, 8, pool_step, jnp.zeros((QT, 128), F32))
    act[...] = acc[...] / jnp.sum(cnt, -1, keepdims=True) + cond[...].astype(F32)

    nvalid = jnp.sum(
        jnp.sum(mask[...].astype(F32), 1, keepdims=True), 0, keepdims=True
    )
    lane = iota((1, 128), 1)
    lanef = lane.astype(F32)
    mine = 2 * r + k

    def kv_slot(b, s):
        return kv.at[b, s, :, 0:QT, :]

    pend = []
    for b in range(2):
        n = normed(act[...]).astype(BF16)
        kv[b, mine, 0, 0:QT, :] = dot(n, wq[4 * b + 1]).astype(BF16)
        kv[b, mine, 1, 0:QT, :] = dot(n, wq[4 * b + 2]).astype(BF16)
        for j in range(1, NR):
            cp = rcopy(
                kv_slot(b, mine),
                kv_slot(b, mine),
                kv_ss.at[b, j],
                kv_rs.at[b, mine],
                ((r + j) % NR, c),
            )
            cp.start()
            pend.append(cp)
        fwd = []
        for j in range(NR):
            s = 2 * ((r + j) % NR) + k
            fwd.append(
                rcopy(kv_slot(b, s), kv_slot(b, s), kv_ss.at[b, NR + j], kv_rs.at[b, s], sib)
            )
        fwd[0].start()
        pend += fwd
        q = dot(n, wq[4 * b]).astype(BF16).astype(F32)
        gate = dot(n, wq[4 * b + 3])
        lq = iota((QT, 128), 1)
        qs = jnp.concatenate(
            [
                jnp.where(lq < 48, q, 0.0),
                jnp.where(lq < 48, 0.0, q),
            ],
            0,
        ).astype(BF16)
        b_own[b].wait()
        for j in range(1, NC):
            s = (c + j) % NC
            rcopy(bb.at[b, s], bb.at[b, s], b_ss.at[b, 0], b_rs.at[b, s], sib).wait_recv()
        for j in range(1, NR):
            s = 2 * ((r + j) % NR) + k
            rcopy(kv_slot(b, s), kv_slot(b, s), kv_ss.at[b, 0], kv_rs.at[b, s], sib).wait_recv()
            fwd[j].start()
        for j in range(NR):
            s = 2 * ((r + j) % NR) + 1 - k
            rcopy(kv_slot(b, s), kv_slot(b, s), kv_ss.at[b, 0], kv_rs.at[b, s], sib).wait_recv()
        if b == 0:
            for cp in b_send[1]:
                cp.start()

        def score_step(s2, mx):
            keys = jnp.concatenate([kv[b, 2 * s2, 0], kv[b, 2 * s2 + 1, 0]], 0)
            s = dot_t(qs, keys) * (1.0 / math.sqrt(48.0))
            for d in range(2):
                slot = 2 * s2 + d
                first = (QT * slot).astype(F32)
                ok = lanef + first < jnp.minimum(nvalid, first + QT)
                parts = []
                for h in range(2):
                    m = bb[b, slot, h]
                    tail = jnp.where(
                        lane < 32,
                        pltpu.roll(m[0:24], 32, 1),
                        jnp.where(
                            lane < 64, pltpu.roll(m[24:48], 64, 1), pltpu.roll(m[48:72], 96, 1)
                        ),
                    )
                    parts += [m, tail]
                sc = jnp.where(ok, s[:, 128 * d : 128 * d + 128] + jnp.concatenate(parts, 0), NEG)
                ssc[slot] = sc
                mx = jnp.maximum(mx, sc)
            return mx

        mx = lax.fori_loop(0, 8, score_step, jnp.full((2 * QT, 128), 2 * NEG, F32))
        top = jnp.max(mx, -1, keepdims=True)

        def value_step(s2, state):
            tot, o = state
            e0 = jnp.exp(ssc[2 * s2] - top)
            e1 = jnp.exp(ssc[2 * s2 + 1] - top)
            p = jnp.concatenate([e0, e1], 1).astype(BF16)
            vals = jnp.concatenate([kv[b, 2 * s2, 1], kv[b, 2 * s2 + 1, 1]], 0)
            return tot + (e0 + e1), o + dot(p, vals)

        zero = jnp.zeros((2 * QT, 128), F32)
        tot, o = lax.fori_loop(0, 8, value_step, (zero, zero))
        o = o / jnp.sum(tot, -1, keepdims=True)
        o = jnp.where(lq < 48, o[:QT], o[QT:])
        ob[b, i] = (jax.nn.sigmoid(gate) * o).astype(BF16)
        for j in range(1, NCH):
            cp = rcopy(ob.at[b, i], ob.at[b, i], o_ss.at[b, j], o_rs.at[b, i], chip(j))
            cp.start()
            pend.append(cp)
        if b == 0:
            for cp in ld_tok:
                cp.wait()
            for cp in swap:
                cp.wait_recv()
        for j in range(1, NCH):
            s = (i + j) % NCH
            rcopy(ob.at[b, s], ob.at[b, s], o_ss.at[b, 0], o_rs.at[b, s], sib).wait_recv()
        gated = jnp.concatenate([ob[b, s] for s in range(NCH)], 1)
        act[...] += dot(gated, topad[8 * b : 8 * b + 8].reshape(1024, 768))

        m = normed(act[...]).astype(BF16)
        part = jnp.zeros((QT, 768), F32)
        for s in range(2):
            swish = jax.nn.silu(dot(m, tin[s, b, 0]))
            hidden = (swish * dot(m, tin[s, b, 1])).astype(BF16)
            part = part + dot(hidden, tout[s, b])
        prt[b] = part.astype(BF16)
        for o_ in range(OWN):

            @pl.when(i != o_)
            def _():
                rcopy(
                    prt.at[b, 16 * o_ : 16 * o_ + 16],
                    rsb.at[b, i],
                    r_ss.at[b, o_],
                    r_rs.at[b, i],
                    (r, 2 * o_ + k),
                ).start()

        @pl.when(is_owner)
        def _():
            row0 = pl.multiple_of(16 * i, 16)
            rsb[b, i] = prt[b, pl.ds(row0, 16), :]
            for j in range(1, NCH):
                s = (i + j) % NCH
                rcopy(rsb.at[b, s], rsb.at[b, s], r_ss.at[b, 0], r_rs.at[b, s], sib).wait_recv()
            total = rsb[b, 0].astype(F32)
            for s in range(1, NCH):
                total = total + rsb[b, s].astype(F32)
            if b == 0:
                db[i] = total.astype(BF16)
                for j in range(1, NCH):
                    rcopy(db.at[i], db.at[i], d_ss.at[j], d_rs.at[i], chip(j)).start()
            else:
                last = act[pl.ds(row0, 16), :] + total
                here = pl.multiple_of(64 + QT * k + 16 * i, 16)
                mine_p = proj.at[pl.ds(here, 16)]
                proj[pl.ds(here, 16), :] = dot(
                    normed(last).astype(BF16), tok_atom[...]
                ).astype(BF16)
                for j in range(1, NC):
                    rcopy(
                        mine_p, mine_p, p_ss.at[j], p_rs.at[OWN * k + i], (r, (c + j) % NC)
                    ).start()

                @pl.when(is_tail)
                def _():
                    rcopy(
                        mine_p,
                        proj.at[pl.ds(pl.multiple_of(16 * (i - 2), 16), 16)],
                        p_ss.at[16],
                        p_rs.at[10 + i],
                        ((r + 1) % NR, 0),
                    ).start()

                @pl.when(is_head)
                def _():
                    rcopy(
                        mine_p,
                        proj.at[pl.ds(pl.multiple_of(256 + 16 * i, 16), 16)],
                        p_ss.at[16],
                        p_rs.at[12 + i],
                        ((r + NR - 1) % NR, NC - 1),
                    ).start()

        if b == 0:
            for o_ in range(OWN):

                @pl.when(i != o_)
                def _():
                    rcopy(db.at[o_], db.at[o_], d_ss.at[0], d_rs.at[o_], sib).wait_recv()

            act[...] += jnp.concatenate([db[s].astype(F32) for s in range(OWN)], 0)

    for cp in edge:
        cp.wait_recv()
    half = iota((1, 128), 1) < 64
    high = xe[0, 0:16, :].astype(F32)[0:1] + jnp.where(c == NC - 1, 192.0, 0.0)
    low = xe[1, 64:80, :].astype(F32)[0:1] - jnp.where(c == 0, 192.0, 0.0)
    side = jnp.where(half, high, low) + 64.0
    tcol = jnp.concatenate(
        [
            jnp.transpose(jnp.broadcast_to(tokrow + 64.0, (128, 128))),
            jnp.transpose(jnp.broadcast_to(side, (128, 128))),
        ],
        0,
    )
    lane2 = iota((256, 128), 1).astype(F32)
    hot = jnp.concatenate(
        [jnp.where(tcol == lane2 + 128.0 * t, 1.0, 0.0) for t in range(3)], 1
    ).astype(BF16)
    x1cat = jnp.concatenate([x1all[c, 16:144, :], xe[0, 16:80, :], xe[1, 0:64, :]], 0).astype(F32)

    def proj_wait(slot, row, n):
        ref = proj.at[row : row + n]
        rcopy(ref, ref, p_ss.at[0], p_rs.at[slot], sib).wait_recv()

    for s in range(2 * OWN):

        @pl.when(jnp.logical_or(i >= OWN, s != OWN * k + i))
        def _():
            proj_wait(s, 64 + 16 * s, 16)

    @pl.when(c == 0)
    def _():
        for s in range(4):
            proj_wait(12 + s, 16 * s, 16)

    @pl.when(c == NC - 1)
    def _():
        for s in range(4):
            proj_wait(12 + s, 256 + 16 * s, 16)

    spread = dot(hot, proj[...])
    x2 = (x1cat + spread).astype(BF16).astype(F32)
    x3 = atom_layer(x2, valid, dec_in, dec_out)
    n3 = normed(x3.astype(F32)).astype(BF16)
    out[...] = dot_t(pos[...], n3)

    for cp in halo + swap + edge + x_send + x_fwd + b_send[0] + b_send[1] + pend:
        cp.wait_send()
    for b in range(2):
        for o_ in range(OWN):

            @pl.when(i != o_)
            def _():
                src = prt.at[b, 16 * o_ : 16 * o_ + 16]
                rcopy(src, rsb.at[b, i], r_ss.at[b, o_], r_rs.at[b, i], sib).wait_send()

    @pl.when(is_owner)
    def _():
        for j in range(1, NCH):
            rcopy(db.at[i], db.at[i], d_ss.at[j], d_rs.at[i], sib).wait_send()
        ref = proj.at[pl.ds(pl.multiple_of(64 + QT * k + 16 * i, 16), 16)]
        for j in range(1, NC):
            rcopy(ref, ref, p_ss.at[j], p_rs.at[0], sib).wait_send()

        @pl.when(jnp.logical_or(is_tail, is_head))
        def _():
            rcopy(ref, ref, p_ss.at[16], p_rs.at[0], sib).wait_send()


def body(
    atom_feat,
    atom_token,
    window_start,
    token_cond,
    token_mask,
    pair,
    enc_in,
    enc_out,
    pool_weight,
    tok_in,
    tok_out,
    pair_weight,
    trans_in,
    trans_out,
    tok_atom,
    dec_in,
    dec_out,
    pos_out,
):
    vm = pl.BlockSpec(memory_space=pltpu.VMEM)
    hb = pl.BlockSpec(memory_space=pl.ANY)
    dma = pltpu.SemaphoreType.DMA
    wt = jnp.transpose(pair_weight, (0, 2, 1)).reshape(32, 128)
    V = pltpu.VMEM
    scratch = [
        V((QT, 768), BF16),
        V((192, 96, 128), BF16),
        V((4, 128, 128), BF16),
        V((128, 128), BF16),
        V((128, 768), BF16),
        V((8, 768, 256), BF16),
        V((8, 768, 128), BF16),
        V((16, 128, 768), BF16),
        V((2, 2, 2, 768, 96), BF16),
        V((2, 2, 96, 768), BF16),
        V((768, 128), BF16),
        V((4, 128, 128), BF16),
        V((128, 128), BF16),
        V((3, 128), BF16),
        V((2, 64, 128), BF16),
        V((16, 160, 128), BF16),
        V((2, 80, 128), BF16),
        V((32, 144, 128), F32),
        V((2, 16, 2, 72, 128), F32),
        V((2, 16, 2, 128, 128), BF16),
        V((16, 192, 128), F32),
        V((2, 8, QT, 128), BF16),
        V((2, QT, 768), BF16),
        V((2, 8, 16, 768), BF16),
        V((6, 16, 768), BF16),
        V((QT, 768), F32),
        V((QT, 768), F32),
        V((384, 128), BF16),
        dma((24,)),
        dma((2,)),
        dma((2,)),
        dma((16,)),
        dma((16,)),
        dma((2,)),
        dma((2,)),
        dma((2,)),
        dma((2,)),
        dma((2, 16)),
        dma((2, 16)),
        dma((2, 16)),
        dma((2, 16)),
        dma((2, 8)),
        dma((2, 8)),
        dma((2, 8)),
        dma((2, 8)),
        dma((8,)),
        dma((8,)),
        dma((17,)),
        dma((16,)),
    ]
    return pl.pallas_call(
        kernel,
        out_shape=jax.ShapeDtypeStruct((3, 128), F32),
        in_specs=[pl.BlockSpec(memory_space=pltpu.SMEM)] + [vm] * 4 + [hb] * 13,
        out_specs=vm,
        scratch_shapes=scratch,
        compiler_params=pltpu.CompilerParams(
            collective_id=0, has_side_effects=True, vmem_limit_bytes=56 << 20
        ),
        name="diffusion_step",
    )(
        window_start,
        atom_token.reshape(1, 128),
        token_mask.reshape(12, 128),
        atom_feat,
        wt,
        token_cond,
        pair,
        enc_in,
        enc_out,
        pool_weight,
        tok_in.reshape(8, 768, 768),
        tok_out.reshape(16, 96, 768),
        trans_in,
        trans_out,
        tok_atom,
        dec_in,
        dec_out,
        pos_out,
    )


def solution(mesh):
    in_specs = (
        P(("row", "col"), None),
        P(("row", "col")),
        P(("row", "col")),
        P("row", None),
        P(),
        P("row", "col", None),
        P(),
        P(),
        P(),
        P(),
        P(),
        P(),
        P(None, None, None, "col"),
        P(None, "col", None),
        P(),
        P(),
        P(),
        P(),
    )
    out_specs = P(None, ("row", "col"))
    return jax.shard_map(body, mesh=mesh, in_specs=in_specs, out_specs=out_specs, check_vma=False)
```

```python
import math

import jax
import jax.numpy as jnp
from jax import lax
from jax.experimental import pallas as pl
from jax.experimental.pallas import tpu as pltpu
from jax.sharding import PartitionSpec as P

MESH = pl.DeviceIdType.MESH
F32 = jnp.float32
BF16 = jnp.bfloat16
NEG = -1000000000.0
NR = 8
NC = 16
NCH = 8
OWN = 6
QT = 96
BT = 8


def dot(a, b):
    return jnp.dot(a, b, preferred_element_type=F32)


def dot_t(a, b):
    return lax.dot_general(a, b, (((1,), (1,)), ((), ())), preferred_element_type=F32)


def normed(x):
    cent = x - jnp.mean(x, -1, keepdims=True)
    var = jnp.mean(cent * cent, -1, keepdims=True)
    return cent * lax.rsqrt(var + 1e-05)


def iota(shape, dim):
    return lax.broadcasted_iota(jnp.int32, shape, dim)


def atom_layer(xf, valid, w_in, w_out):
    n = normed(xf).astype(BF16)
    own = n[:128]
    q = dot(own, w_in[0]).astype(BF16).astype(F32)
    keys = dot(n, w_in[1]).astype(BF16)
    vals = dot(n, w_in[2]).astype(BF16)
    gate = dot(own, w_in[3])
    head = iota((128, 128), 1) // 32
    outs = jnp.zeros((128, 128), F32)
    for h in range(4):
        qh = jnp.where(head == h, q, 0.0).astype(BF16)
        s = dot_t(qh, keys) * (1.0 / math.sqrt(32.0))
        s = jnp.where(valid, s, NEG)
        e = jnp.exp(s - jnp.max(s, -1, keepdims=True))
        total = jnp.sum(e, -1, keepdims=True)
        o = dot(e.astype(BF16), vals) / total
        outs = jnp.where(head == h, o, outs)
    gated = (jax.nn.sigmoid(gate) * outs).astype(BF16)
    return (xf[:128] + dot(gated, w_out[...])).astype(BF16)


def kernel(
    ws,
    tok,
    mask,
    x_in,
    wt,
    cond_h,
    pair_h,
    enc_in_h,
    enc_out_h,
    pool_h,
    tok_in_h,
    tok_out_h,
    tin_h,
    tout_h,
    tok_atom_h,
    dec_in_h,
    dec_out_h,
    pos_h,
    out,
    cond,
    pair,
    enc_in,
    enc_out,
    pool,
    slab,
    wq,
    topad,
    tin,
    tout,
    tok_atom,
    dec_in,
    dec_out,
    pos,
    xh,
    x1all,
    xe,
    zb,
    bb,
    kv,
    ssc,
    ob,
    prt,
    rsb,
    db,
    act,
    feats,
    hots,
    proj,
    lsem,
    h_ss,
    h_rs,
    x_ss,
    x_rs,
    e_ss,
    e_rs,
    t_ss,
    t_rs,
    b_ss,
    b_rs,
    kv_ss,
    kv_rs,
    o_ss,
    o_rs,
    r_ss,
    r_rs,
    d_ss,
    d_rs,
    p_ss,
    p_rs,
):
    r = lax.axis_index("row")
    c = lax.axis_index("col")
    i = c // 2
    k = c % 2
    sib = (r, c + 1 - 2 * k)
    flat = r * NC + c
    nxt = (flat + 1) % (NR * NC)
    prv = (flat + NR * NC - 1) % (NR * NC)
    nxt = (nxt // NC, nxt % NC)
    prv = (prv // NC, prv % NC)
    is_owner = i < OWN
    is_tail = jnp.logical_and(k == 1, jnp.logical_and(i >= 2, i < OWN))
    is_head = jnp.logical_and(k == 0, i < 4)

    def chip(j):
        return (r, 2 * ((i + j) % NCH) + k)

    def rcopy(src, dst, ss, rs, dev):
        return pltpu.make_async_remote_copy(
            src_ref=src, dst_ref=dst, send_sem=ss, recv_sem=rs, device_id=dev, device_id_type=MESH
        )

    nload = [0]

    def load(src, dst):
        cp = pltpu.make_async_copy(src, dst, lsem.at[nload[0]])
        nload[0] += 1
        cp.start()
        return cp

    ld_pair = [load(pair_h.at[48 * j : 48 * j + 48], pair.at[48 * j : 48 * j + 48]) for j in range(4)]
    ld_enc = [load(enc_in_h, enc_in), load(enc_out_h, enc_out)]
    ld_pool = [
        load(pool_h, pool),
        load(cond_h.at[pl.ds(pl.multiple_of(QT * k, 32), QT)], cond),
    ]
    base = jnp.minimum(128 * ((QT * i) // 128), 512)
    base = pl.multiple_of(base, 128)
    shift = QT * i - base
    ld_slab = [load(tok_in_h.at[:, :, pl.ds(base, 256)], slab)]
    core_rows = pl.ds(pl.multiple_of(QT * k, 32), QT)
    tin_k = tin.at[:, :, core_rows, :]
    tout_k = tout.at[:, core_rows, :]
    ld_tok = [
        load(tok_out_h.at[:, 32:96], topad.at[:, 0:64]),
        load(tok_out_h.at[:, 0:32], topad.at[:, 96:128]),
        load(tin_h, tin_k),
        load(tout_h, tout_k),
        load(tok_atom_h, tok_atom),
        load(dec_in_h, dec_in),
        load(dec_out_h, dec_out),
        load(pos_h, pos),
    ]

    topad[:, 64:96, :] = jnp.zeros((16, 32, 768), BF16)
    proj[...] = jnp.zeros((384, 128), BF16)

    bar = pltpu.get_barrier_semaphore()

    def greet(dev):
        pl.semaphore_signal(bar, inc=1, device_id=dev, device_id_type=MESH)

    for j in range(1, NC):
        greet((r, (c + j) % NC))
    for j in range(1, NR):
        greet(((r + j) % NR, c))
    greet(nxt)
    greet(prv)

    @pl.when(c == 0)
    def _():
        for o in (5, 7, 9, 11):
            greet(((r + NR - 1) % NR, o))

    @pl.when(c == NC - 1)
    def _():
        for o in (0, 2, 4, 6):
            greet(((r + 1) % NR, o))

    extra = jnp.where(jnp.logical_or(is_tail, is_head), 1, 0)
    pl.semaphore_wait(bar, 24 + extra)

    halo = [
        rcopy(x_in.at[64:128], xh.at[1], h_ss.at[0], h_rs.at[1], nxt),
        rcopy(x_in.at[0:64], xh.at[0], h_ss.at[1], h_rs.at[0], prv),
    ]
    for cp in halo:
        cp.start()
    swap = [
        rcopy(tin_h, tin_k, t_ss.at[0], t_rs.at[0], sib),
        rcopy(tout_h, tout_k, t_ss.at[1], t_rs.at[1], sib),
    ]
    for cp in swap:
        cp.start()

    def bias_half(kp):
        w = wt[...]
        for kb in range(3):

            @pl.loop(0, 24 // BT)
            def _(u):
                t = 24 * kb + BT * u
                rows = []
                for d in range(BT):
                    rows.append(pair[QT * kp + t + d])
                    rows.append(pair[QT * kp + 72 + BT * u + d, 32 * kb : 32 * kb + 32, :])
                res = dot_t(w, jnp.concatenate(rows, 0))
                zf = zb.reshape(32 * 144, 128)
                for d in range(BT):
                    for g in range(4):
                        zf[pl.ds(g * 8 * 144 + kp * 72 + t + d, 8, stride=144), :] = res[
                            8 * g : 8 * g + 8, 128 * d : 128 * d + 128
                        ]

    def bias_src(b, ch, core):
        return zb.at[pl.ds(16 * b + 2 * ch, 2), pl.ds(pl.multiple_of(72 * core, 8), 72), :]

    def bias_send(b, j, core):
        ch = (i + j) % NCH
        return rcopy(
            bias_src(b, ch, core), bb.at[b, c], b_ss.at[b, 2 * j + core], b_rs.at[b, c], (r, 2 * ch + core)
        )

    def bias_sib(b):
        return rcopy(bias_src(b, i, 1 - k), bb.at[b, c], b_ss.at[b, 0], b_rs.at[b, c], sib)

    ld_pair[0].wait()
    ld_pair[1].wait()
    bias_half(0)

    for cp in ld_enc:
        cp.wait()
    for cp in halo:
        cp.wait_recv()
    rowi = iota((128, 256), 0)
    coli = iota((128, 256), 1)
    glob = flat * 128 + jnp.where(coli < 192, coli, coli - 256)
    start = jnp.where(
        rowi < 64, jnp.where(rowi < 32, ws[0], ws[1]), jnp.where(rowi < 96, ws[2], ws[3])
    )
    start = jnp.maximum(start, 0)
    stop = jnp.where(
        rowi < 64, jnp.where(rowi < 32, ws[0], ws[1]), jnp.where(rowi < 96, ws[2], ws[3])
    ) + 128
    stop = jnp.minimum(stop, NR * NC * 128)
    valid = jnp.logical_and(glob >= start, glob < stop)
    xf = jnp.concatenate([x_in[...], xh[0], xh[1]], 0).astype(F32)
    x1 = atom_layer(xf, valid, enc_in, enc_out)
    tokrow = (tok[...] - 192 * r).astype(F32)
    tokrows = jnp.broadcast_to(tokrow, (16, 128)).astype(BF16)
    x1all[c, 0:16, :] = tokrows
    x1all[c, 16:144, :] = x1
    x1all[c, 144:160, :] = tokrows

    edge = [
        rcopy(x1all.at[c, 80:160], xe.at[1], e_ss.at[0], e_rs.at[1], nxt),
        rcopy(x1all.at[c, 0:80], xe.at[0], e_ss.at[1], e_rs.at[0], prv),
    ]

    def x1_slot(s):
        return x1all.at[s, 0:144]

    x_send = [
        rcopy(x1_slot(c), x1_slot(c), x_ss.at[j], x_rs.at[c], chip(j)) for j in range(1, NCH)
    ]
    x_fwd = []
    for j in range(NCH):
        s = 2 * ((i + j) % NCH) + k
        x_fwd.append(rcopy(x1_slot(s), x1_slot(s), x_ss.at[NCH + j], x_rs.at[s], sib))
    x_far = []
    for j in range(NCH):
        s = 2 * ((i + j) % NCH) + 1 - k
        x_far.append(rcopy(x1_slot(s), x1_slot(s), x_ss.at[NCH + j], x_rs.at[s], sib))
    for cp in x_send:
        cp.start()
    x_fwd[0].start()
    for cp in edge:
        cp.start()

    b_send = [[], []]
    for j in range(1, NCH):
        b_send[0].append(bias_send(0, j, 0))
        b_send[0][-1].start()
    ld_pair[2].wait()
    ld_pair[3].wait()
    bias_half(1)
    for j in range(1, NCH):
        b_send[0].append(bias_send(0, j, 1))
        b_send[0][-1].start()
    b_send[0].append(bias_sib(0))
    b_send[0][-1].start()
    for j in range(1, NCH):
        for core in range(2):
            b_send[1].append(bias_send(1, j, core))
    b_send[1].append(bias_sib(1))
    b_own = []
    for b in range(2):
        cp = pltpu.make_async_copy(bias_src(b, i, k), bb.at[b, c], lsem.at[nload[0] + b])
        cp.start()
        b_own.append(cp)
    bulk = list(b_send[1])

    def some_bulk(n):
        for _ in range(n):
            if bulk:
                bulk.pop(0).start()

    for cp in ld_slab:
        cp.wait()
    e_row = iota((256, 256), 0) - shift
    e_col = iota((256, 256), 1)

    def picker(lo, hi, first):
        hit = jnp.logical_and(e_col >= lo, e_col < hi)
        return jnp.logical_and(hit, e_row == e_col - lo + first)

    def onehot(m):
        return jnp.where(m, 1.0, 0.0).astype(BF16)

    pick_q = onehot(picker(0, 96, 0))
    pick_g = onehot(jnp.logical_or(picker(128, 192, 32), picker(224, 256, 0)))
    pick_k = onehot(picker(0, 96, 0))
    pick_v = onehot(picker(96, 192, 0))

    @pl.loop(0, 2)
    def _(m):
        wq[2 * m] = (dot(slab[4 * m], pick_q) + dot(slab[4 * m + 3], pick_g)).astype(BF16)
        wq[2 * m + 1] = (dot(slab[4 * m + 1], pick_k) + dot(slab[4 * m + 2], pick_v)).astype(BF16)

    for cp in ld_pool:
        cp.wait()
    want = (iota((QT, 128), 0) + QT * k).astype(F32)

    def pool_slot(s):
        feats[s] = jnp.maximum(dot(x1all[s, 16:144, :], pool[...]), 0.0).astype(BF16)
        t = x1all[s, 0:16, :].astype(F32)[0:1]
        hots[s] = jnp.where(t == want, 1.0, 0.0).astype(BF16)

    pool_slot(c)
    for j in range(1, NCH):
        s = 2 * ((i + j) % NCH) + k
        rcopy(x1_slot(s), x1_slot(s), x_ss.at[0], x_rs.at[s], sib).wait_recv()
        x_fwd[j].start()
        pool_slot(s)
    for j in range(NCH):
        x_far[j].wait_recv()
        pool_slot(2 * ((i + j) % NCH) + 1 - k)
    hot_all = jnp.concatenate([hots[s] for s in range(NC)], 1)
    cnt = hots[0].astype(F32)
    for s in range(1, NC):
        cnt = cnt + hots[s].astype(F32)
    sums = dot(hot_all, feats[...].reshape(NC * 128, 768))
    act[...] = sums / jnp.sum(cnt, -1, keepdims=True) + cond[...].astype(F32)

    nvalid = jnp.sum(
        jnp.sum(mask[...].astype(F32), 1, keepdims=True), 0, keepdims=True
    )
    lane = iota((1, 128), 1)
    lanef = lane.astype(F32)
    mine = 2 * r + k

    left = jnp.where(lane < 64, 1.0, 0.0).astype(BF16)
    right = jnp.where(lane < 64, 0.0, 1.0).astype(BF16)
    pad = jnp.zeros((32, 128), BF16)
    lq = iota((QT, 128), 1)

    def kv_slot(b, s):
        return kv.at[b, s]

    pend = []
    for b in range(2):
        n = normed(act[...]).astype(BF16)
        own_kv = dot(n, wq[2 * b + 1])
        kv[b, mine, 0] = own_kv[0:48, 0:128].astype(BF16)
        kv[b, mine, 1] = jnp.where(
            lane < 64, own_kv[0:48, 128:256], pltpu.roll(own_kv[48:96, 128:256], 64, 1)
        ).astype(BF16)
        kv[b, mine, 2] = own_kv[48:96, 0:128].astype(BF16)
        for j in range(1, NR):
            cp = rcopy(
                kv_slot(b, mine),
                kv_slot(b, mine),
                kv_ss.at[b, j],
                kv_rs.at[b, mine],
                ((r + j) % NR, c),
            )
            cp.start()
            pend.append(cp)
        fwd = []
        for j in range(NR):
            s = 2 * ((r + j) % NR) + k
            fwd.append(
                rcopy(kv_slot(b, s), kv_slot(b, s), kv_ss.at[b, NR + j], kv_rs.at[b, s], sib)
            )
        fwd[0].start()
        pend += fwd
        qg = dot(n, wq[2 * b])
        q = qg[:, 0:128].astype(BF16).astype(F32)
        gate = jax.nn.sigmoid(qg[:, 128:256])
        qs = jnp.concatenate([jnp.where(lq < 48, q, 0.0), jnp.where(lq < 48, 0.0, q)], 0).astype(
            BF16
        )
        b_own[b].wait()
        for j in range(1, NC):
            s = (c + j) % NC
            rcopy(bb.at[b, s], bb.at[b, s], b_ss.at[b, 0], b_rs.at[b, s], sib).wait_recv()

        def scores(slots, mx):
            keys = []
            for s in slots:
                keys += [kv[b, s, 0], kv[b, s, 2], pad]
            dots = dot_t(qs, jnp.concatenate(keys, 0)) * (1.0 / math.sqrt(48.0))
            for d, slot in enumerate(slots):
                first = (QT * slot).astype(F32)
                ok = lanef + first < jnp.minimum(nvalid, first + QT)
                parts = []
                for h in range(2):
                    m = bb[b, slot, h]
                    tail = jnp.where(
                        lane < 32,
                        pltpu.roll(m[0:24], 32, 1),
                        jnp.where(
                            lane < 64, pltpu.roll(m[24:48], 64, 1), pltpu.roll(m[48:72], 96, 1)
                        ),
                    )
                    parts += [m, tail]
                sc = dots[:, 128 * d : 128 * d + 128] + jnp.concatenate(parts, 0)
                sc = jnp.where(ok, sc, NEG)
                ssc[slot] = sc
                mx = jnp.maximum(mx, sc)
            return mx

        mx = jnp.full((2 * QT, 128), 2 * NEG, F32)
        for grp in range(4):
            slots = []
            for j in (2 * grp, 2 * grp + 1):
                s = 2 * ((r + j) % NR) + k
                slots.append(s)
                if j > 0:
                    rcopy(
                        kv_slot(b, s), kv_slot(b, s), kv_ss.at[b, 0], kv_rs.at[b, s], sib
                    ).wait_recv()
                    fwd[j].start()
            for j in (2 * grp, 2 * grp + 1):
                s = 2 * ((r + j) % NR) + 1 - k
                slots.append(s)
                rcopy(kv_slot(b, s), kv_slot(b, s), kv_ss.at[b, 0], kv_rs.at[b, s], sib).wait_recv()
            mx = scores(slots, mx)
        if b == 0:
            some_bulk(3)
        top = jnp.max(mx, -1, keepdims=True)

        def value_step(s4, state):
            tot, o = state
            ps = []
            vals = []
            for d in range(4):
                s = 4 * s4 + d
                e = jnp.exp(ssc[s] - top)
                tot = tot + e
                ps.append(e.astype(BF16))
                mid = kv[b, s, 1]
                vals.append(jnp.concatenate([kv[b, s, 0], mid * left], 1))
                vals.append(jnp.concatenate([kv[b, s, 2], mid * right], 1))
                vals.append(jnp.concatenate([pad, pad], 1))
            return tot, o + dot(jnp.concatenate(ps, 1), jnp.concatenate(vals, 0))

        tot, o = lax.fori_loop(
            0, 4, value_step, (jnp.zeros((2 * QT, 128), F32), jnp.zeros((2 * QT, 256), F32))
        )
        inv = 1.0 / jnp.sum(tot, -1, keepdims=True)
        o_a = o[:QT, 0:128] * inv[:QT]
        o_b = (o[:, 128:256] + pltpu.roll(o[:, 128:256], 64, 1)) * inv
        o = jnp.where(lq < 16, o_b[:QT], jnp.where(lq < 64, o_b[QT:], jnp.where(lq < 96, 0.0, o_a)))
        ob[b, i] = (gate * o).astype(BF16)
        for j in range(1, NCH):
            cp = rcopy(ob.at[b, i], ob.at[b, i], o_ss.at[b, j], o_rs.at[b, i], chip(j))
            cp.start()
            pend.append(cp)
        if b == 0:
            some_bulk(4)
            for cp in ld_tok:
                cp.wait()
            for cp in swap:
                cp.wait_recv()
        for j in range(1, NCH):
            s = (i + j) % NCH
            rcopy(ob.at[b, s], ob.at[b, s], o_ss.at[b, 0], o_rs.at[b, s], sib).wait_recv()
        gated = jnp.concatenate([ob[b, s] for s in range(NCH)], 1)
        act[...] += dot(gated, topad[8 * b : 8 * b + 8].reshape(1024, 768))

        m = normed(act[...]).astype(BF16)
        swish = jax.nn.silu(dot_t(m, tin[b, 0]))
        hidden = (swish * dot_t(m, tin[b, 1])).astype(BF16)
        prt[b] = dot(hidden, tout[b]).astype(BF16)
        for o_ in range(OWN):

            @pl.when(i != o_)
            def _():
                rcopy(
                    prt.at[b, 16 * o_ : 16 * o_ + 16],
                    rsb.at[b, i],
                    r_ss.at[b, o_],
                    r_rs.at[b, i],
                    (r, 2 * o_ + k),
                ).start()

        if b == 0:
            some_bulk(4)

        @pl.when(is_owner)
        def _():
            row0 = pl.multiple_of(16 * i, 16)
            rsb[b, i] = prt[b, pl.ds(row0, 16), :]
            for j in range(1, NCH):
                s = (i + j) % NCH
                rcopy(rsb.at[b, s], rsb.at[b, s], r_ss.at[b, 0], r_rs.at[b, s], sib).wait_recv()
            total = rsb[b, 0].astype(F32)
            for s in range(1, NCH):
                total = total + rsb[b, s].astype(F32)
            if b == 0:
                db[i] = total.astype(BF16)
                for j in range(1, NCH):
                    rcopy(db.at[i], db.at[i], d_ss.at[j], d_rs.at[i], chip(j)).start()
            else:
                last = act[pl.ds(row0, 16), :] + total
                here = pl.multiple_of(64 + QT * k + 16 * i, 16)
                mine_p = proj.at[pl.ds(here, 16)]
                proj[pl.ds(here, 16), :] = dot(
                    normed(last).astype(BF16), tok_atom[...]
                ).astype(BF16)
                for j in range(1, NC):
                    rcopy(
                        mine_p, mine_p, p_ss.at[j], p_rs.at[OWN * k + i], (r, (c + j) % NC)
                    ).start()

                @pl.when(is_tail)
                def _():
                    rcopy(
                        mine_p,
                        proj.at[pl.ds(pl.multiple_of(16 * (i - 2), 16), 16)],
                        p_ss.at[16],
                        p_rs.at[10 + i],
                        ((r + 1) % NR, 0),
                    ).start()

                @pl.when(is_head)
                def _():
                    rcopy(
                        mine_p,
                        proj.at[pl.ds(pl.multiple_of(256 + 16 * i, 16), 16)],
                        p_ss.at[16],
                        p_rs.at[12 + i],
                        ((r + NR - 1) % NR, NC - 1),
                    ).start()

        if b == 0:
            some_bulk(4)
            for o_ in range(OWN):

                @pl.when(i != o_)
                def _():
                    rcopy(db.at[o_], db.at[o_], d_ss.at[0], d_rs.at[o_], sib).wait_recv()

            act[...] += jnp.concatenate([db[s].astype(F32) for s in range(OWN)], 0)

    for cp in edge:
        cp.wait_recv()
    half = iota((1, 128), 1) < 64
    high = xe[0, 0:16, :].astype(F32)[0:1] + jnp.where(c == NC - 1, 192.0, 0.0)
    low = xe[1, 64:80, :].astype(F32)[0:1] - jnp.where(c == 0, 192.0, 0.0)
    side = jnp.where(half, high, low) + 64.0
    tcol = jnp.concatenate(
        [
            jnp.transpose(jnp.broadcast_to(tokrow + 64.0, (128, 128))),
            jnp.transpose(jnp.broadcast_to(side, (128, 128))),
        ],
        0,
    )
    lane2 = iota((256, 128), 1).astype(F32)
    hot = jnp.concatenate(
        [jnp.where(tcol == lane2 + 128.0 * t, 1.0, 0.0) for t in range(3)], 1
    ).astype(BF16)
    x1cat = jnp.concatenate([x1all[c, 16:144, :], xe[0, 16:80, :], xe[1, 0:64, :]], 0).astype(F32)

    def proj_wait(slot, row, n):
        ref = proj.at[row : row + n]
        rcopy(ref, ref, p_ss.at[0], p_rs.at[slot], sib).wait_recv()

    for s in range(2 * OWN):

        @pl.when(jnp.logical_or(i >= OWN, s != OWN * k + i))
        def _():
            proj_wait(s, 64 + 16 * s, 16)

    @pl.when(c == 0)
    def _():
        for s in range(4):
            proj_wait(12 + s, 16 * s, 16)

    @pl.when(c == NC - 1)
    def _():
        for s in range(4):
            proj_wait(12 + s, 256 + 16 * s, 16)

    spread = dot(hot, proj[...])
    x2 = (x1cat + spread).astype(BF16).astype(F32)
    x3 = atom_layer(x2, valid, dec_in, dec_out)
    n3 = normed(x3.astype(F32)).astype(BF16)
    out[...] = dot_t(pos[...], n3)

    for cp in halo + swap + edge + x_send + x_fwd + b_send[0] + b_send[1] + pend:
        cp.wait_send()
    for b in range(2):
        for o_ in range(OWN):

            @pl.when(i != o_)
            def _():
                src = prt.at[b, 16 * o_ : 16 * o_ + 16]
                rcopy(src, rsb.at[b, i], r_ss.at[b, o_], r_rs.at[b, i], sib).wait_send()

    @pl.when(is_owner)
    def _():
        for j in range(1, NCH):
            rcopy(db.at[i], db.at[i], d_ss.at[j], d_rs.at[i], sib).wait_send()
        ref = proj.at[pl.ds(pl.multiple_of(64 + QT * k + 16 * i, 16), 16)]
        for j in range(1, NC):
            rcopy(ref, ref, p_ss.at[j], p_rs.at[0], sib).wait_send()

        @pl.when(jnp.logical_or(is_tail, is_head))
        def _():
            rcopy(ref, ref, p_ss.at[16], p_rs.at[0], sib).wait_send()


def body(
    atom_feat,
    atom_token,
    window_start,
    token_cond,
    token_mask,
    pair,
    enc_in,
    enc_out,
    pool_weight,
    tok_in,
    tok_out,
    pair_weight,
    trans_in,
    trans_out,
    tok_atom,
    dec_in,
    dec_out,
    pos_out,
):
    vm = pl.BlockSpec(memory_space=pltpu.VMEM)
    hb = pl.BlockSpec(memory_space=pl.ANY)
    dma = pltpu.SemaphoreType.DMA
    wt = jnp.transpose(pair_weight, (0, 2, 1)).reshape(32, 128)
    V = pltpu.VMEM
    scratch = [
        V((QT, 768), BF16),
        V((192, 96, 128), BF16),
        V((4, 128, 128), BF16),
        V((128, 128), BF16),
        V((128, 768), BF16),
        V((8, 768, 256), BF16),
        V((4, 768, 256), BF16),
        V((16, 128, 768), BF16),
        V((2, 2, 192, 768), BF16),
        V((2, 192, 768), BF16),
        V((768, 128), BF16),
        V((4, 128, 128), BF16),
        V((128, 128), BF16),
        V((3, 128), BF16),
        V((2, 64, 128), BF16),
        V((16, 160, 128), BF16),
        V((2, 80, 128), BF16),
        V((32, 144, 128), F32),
        V((2, 16, 2, 72, 128), F32),
        V((2, 16, 3, 48, 128), BF16),
        V((16, 192, 128), F32),
        V((2, 8, QT, 128), BF16),
        V((2, QT, 768), BF16),
        V((2, 8, 16, 768), BF16),
        V((6, 16, 768), BF16),
        V((QT, 768), F32),
        V((16, 128, 768), BF16),
        V((16, QT, 128), BF16),
        V((384, 128), BF16),
        dma((24,)),
        dma((2,)),
        dma((2,)),
        dma((16,)),
        dma((16,)),
        dma((2,)),
        dma((2,)),
        dma((2,)),
        dma((2,)),
        dma((2, 16)),
        dma((2, 16)),
        dma((2, 16)),
        dma((2, 16)),
        dma((2, 8)),
        dma((2, 8)),
        dma((2, 8)),
        dma((2, 8)),
        dma((8,)),
        dma((8,)),
        dma((17,)),
        dma((16,)),
    ]
    return pl.pallas_call(
        kernel,
        out_shape=jax.ShapeDtypeStruct((3, 128), F32),
        in_specs=[pl.BlockSpec(memory_space=pltpu.SMEM)] + [vm] * 4 + [hb] * 13,
        out_specs=vm,
        scratch_shapes=scratch,
        compiler_params=pltpu.CompilerParams(
            collective_id=0, has_side_effects=True, vmem_limit_bytes=56 << 20
        ),
        name="diffusion_step",
    )(
        window_start,
        atom_token.reshape(1, 128),
        token_mask.reshape(12, 128),
        atom_feat,
        wt,
        token_cond,
        pair,
        enc_in,
        enc_out,
        pool_weight,
        tok_in.reshape(8, 768, 768),
        tok_out.reshape(16, 96, 768),
        jnp.swapaxes(trans_in, 2, 3),
        trans_out,
        tok_atom,
        dec_in,
        dec_out,
        pos_out,
    )


def solution(mesh):
    in_specs = (
        P(("row", "col"), None),
        P(("row", "col")),
        P(("row", "col")),
        P("row", None),
        P(),
        P("row", "col", None),
        P(),
        P(),
        P(),
        P(),
        P(),
        P(),
        P(None, None, None, "col"),
        P(None, "col", None),
        P(),
        P(),
        P(),
        P(),
    )
    out_specs = P(None, ("row", "col"))
    return jax.shard_map(body, mesh=mesh, in_specs=in_specs, out_specs=out_specs, check_vma=False)
```

```python
import math

import jax
import jax.numpy as jnp
from jax import lax
from jax.experimental import pallas as pl
from jax.experimental.pallas import tpu as pltpu
from jax.sharding import PartitionSpec as P

MESH = pl.DeviceIdType.MESH
F32 = jnp.float32
BF16 = jnp.bfloat16
NEG = -1000000000.0
NR = 8
NC = 16
NCH = 8
OWN = 6
QT = 96
G0, G1, G2 = 5, 4, 4
EARLY = 6
BT = 8


def dot(a, b):
    return jnp.dot(a, b, preferred_element_type=F32)


def dot_t(a, b):
    return lax.dot_general(a, b, (((1,), (1,)), ((), ())), preferred_element_type=F32)


def normed(x):
    cent = x - jnp.mean(x, -1, keepdims=True)
    var = jnp.mean(cent * cent, -1, keepdims=True)
    return cent * lax.rsqrt(var + 1e-05)


def iota(shape, dim):
    return lax.broadcasted_iota(jnp.int32, shape, dim)


def atom_layer(xf, valid, w_in, w_out):
    n = normed(xf).astype(BF16)
    own = n[:128]
    q = dot(own, w_in[0]).astype(BF16).astype(F32)
    keys = dot(n, w_in[1]).astype(BF16)
    vals = dot(n, w_in[2]).astype(BF16)
    gate = dot(own, w_in[3])
    head = iota((128, 128), 1) // 32
    outs = jnp.zeros((128, 128), F32)
    for h in range(4):
        qh = jnp.where(head == h, q, 0.0).astype(BF16)
        s = dot_t(qh, keys) * (1.0 / math.sqrt(32.0))
        s = jnp.where(valid, s, NEG)
        e = jnp.exp(s - jnp.max(s, -1, keepdims=True))
        total = jnp.sum(e, -1, keepdims=True)
        o = dot(e.astype(BF16), vals) / total
        outs = jnp.where(head == h, o, outs)
    gated = (jax.nn.sigmoid(gate) * outs).astype(BF16)
    return (xf[:128] + dot(gated, w_out[...])).astype(BF16)


def kernel(
    ws,
    tok,
    mask,
    x_in,
    wt,
    cond_h,
    pair_h,
    enc_in_h,
    enc_out_h,
    pool_h,
    tok_in_h,
    tok_out_h,
    tin_h,
    tout_h,
    tok_atom_h,
    dec_in_h,
    dec_out_h,
    pos_h,
    out,
    cond,
    pair,
    enc_in,
    enc_out,
    pool,
    slab,
    wq,
    topad,
    tin,
    tout,
    tok_atom,
    dec_in,
    dec_out,
    pos,
    xh,
    x1all,
    xe,
    zb,
    bb,
    kv,
    ssc,
    ob,
    prt,
    rsb,
    db,
    act,
    feats,
    hots,
    proj,
    lsem,
    h_ss,
    h_rs,
    x_ss,
    x_rs,
    e_ss,
    e_rs,
    t_ss,
    t_rs,
    b_ss,
    b_rs,
    kv_ss,
    kv_rs,
    o_ss,
    o_rs,
    r_ss,
    r_rs,
    d_ss,
    d_rs,
    p_ss,
    p_rs,
):
    r = lax.axis_index("row")
    c = lax.axis_index("col")
    i = c // 2
    k = c % 2
    sib = (r, c + 1 - 2 * k)
    flat = r * NC + c
    nxt = (flat + 1) % (NR * NC)
    prv = (flat + NR * NC - 1) % (NR * NC)
    nxt = (nxt // NC, nxt % NC)
    prv = (prv // NC, prv % NC)
    is_owner = i < OWN
    is_tail = jnp.logical_and(k == 1, jnp.logical_and(i >= 2, i < OWN))
    is_head = jnp.logical_and(k == 0, i < 4)

    def chip(j):
        return (r, 2 * ((i + j) % NCH) + k)

    def rcopy(src, dst, ss, rs, dev):
        return pltpu.make_async_remote_copy(
            src_ref=src, dst_ref=dst, send_sem=ss, recv_sem=rs, device_id=dev, device_id_type=MESH
        )

    nload = [0]

    def load(src, dst):
        cp = pltpu.make_async_copy(src, dst, lsem.at[nload[0]])
        nload[0] += 1
        cp.start()
        return cp

    ld_pair = [load(pair_h.at[48 * j : 48 * j + 48], pair.at[48 * j : 48 * j + 48]) for j in range(4)]
    ld_enc = [load(enc_in_h, enc_in), load(enc_out_h, enc_out)]
    ld_pool = [
        load(pool_h, pool),
        load(cond_h.at[pl.ds(pl.multiple_of(QT * k, 32), QT)], cond),
    ]
    base = jnp.minimum(128 * ((QT * i) // 128), 512)
    base = pl.multiple_of(base, 128)
    shift = QT * i - base
    ld_slab = [load(tok_in_h.at[:, :, pl.ds(base, 256)], slab)]
    core_rows = pl.ds(pl.multiple_of(QT * k, 32), QT)
    tin_k = tin.at[:, :, core_rows, :]
    tout_k = tout.at[:, core_rows, :]
    ld_tok = [
        load(tok_out_h.at[:, 32:96], topad.at[:, 0:64]),
        load(tok_out_h.at[:, 0:32], topad.at[:, 96:128]),
        load(tin_h, tin_k),
        load(tout_h, tout_k),
        load(tok_atom_h, tok_atom),
        load(dec_in_h, dec_in),
        load(dec_out_h, dec_out),
        load(pos_h, pos),
    ]

    topad[:, 64:96, :] = jnp.zeros((16, 32, 768), BF16)
    proj[...] = jnp.zeros((384, 128), BF16)

    def bias_half(kp):
        w = wt[...]
        for kb in range(3):

            @pl.loop(0, 24 // BT)
            def _(u):
                t = 24 * kb + BT * u
                rows = []
                for d in range(BT):
                    rows.append(pair[QT * kp + t + d])
                    rows.append(pair[QT * kp + 72 + BT * u + d, 32 * kb : 32 * kb + 32, :])
                res = dot_t(w, jnp.concatenate(rows, 0))
                zf = zb.reshape(32 * 144, 128)
                for d in range(BT):
                    for g in range(4):
                        zf[pl.ds(g * 8 * 144 + kp * 72 + t + d, 8, stride=144), :] = res[
                            8 * g : 8 * g + 8, 128 * d : 128 * d + 128
                        ]

    bar = pltpu.get_barrier_semaphore()

    def greet(dev):
        pl.semaphore_signal(bar, inc=1, device_id=dev, device_id_type=MESH)

    for j in range(1, NC):
        greet((r, (c + j) % NC))
    for j in range(1, NR):
        greet(((r + j) % NR, c))
    greet(nxt)
    greet(prv)

    @pl.when(c == 0)
    def _():
        for o in (5, 7, 9, 11):
            greet(((r + NR - 1) % NR, o))

    @pl.when(c == NC - 1)
    def _():
        for o in (0, 2, 4, 6):
            greet(((r + 1) % NR, o))

    ld_pair[0].wait()
    ld_pair[1].wait()
    bias_half(0)
    extra = jnp.where(jnp.logical_or(is_tail, is_head), 1, 0)
    pl.semaphore_wait(bar, 24 + extra)

    halo = [
        rcopy(x_in.at[64:128], xh.at[1], h_ss.at[0], h_rs.at[1], nxt),
        rcopy(x_in.at[0:64], xh.at[0], h_ss.at[1], h_rs.at[0], prv),
    ]
    for cp in halo:
        cp.start()
    swap = [
        rcopy(tin_h, tin_k, t_ss.at[0], t_rs.at[0], sib),
        rcopy(tout_h, tout_k, t_ss.at[1], t_rs.at[1], sib),
    ]
    for cp in swap:
        cp.start()

    def bias_src(b, ch, core):
        return zb.at[pl.ds(16 * b + 2 * ch, 2), pl.ds(pl.multiple_of(72 * core, 8), 72), :]

    def bias_send(b, j, core):
        ch = (i + j) % NCH
        return rcopy(
            bias_src(b, ch, core), bb.at[b, c], b_ss.at[b, 2 * j + core], b_rs.at[b, c], (r, 2 * ch + core)
        )

    def bias_sib(b):
        return rcopy(bias_src(b, i, 1 - k), bb.at[b, c], b_ss.at[b, 0], b_rs.at[b, c], sib)

    ring = (2, 6, 4, 1, 7, 3, 5)
    b_send = [[], []]
    for b in range(2):
        for core in range(2):
            b_send[b] += [bias_send(b, j, core) for j in ring]
        b_send[b].append(bias_sib(b))
    bulk = b_send[0] + b_send[1]

    def some_bulk(n):
        for _ in range(n):
            if bulk:
                bulk.pop(0).start()

    some_bulk(EARLY)
    ld_pair[2].wait()
    ld_pair[3].wait()
    bias_half(1)
    b_own = []
    for b in range(2):
        cp = pltpu.make_async_copy(bias_src(b, i, k), bb.at[b, c], lsem.at[nload[0] + b])
        cp.start()
        b_own.append(cp)

    for cp in ld_enc:
        cp.wait()
    for cp in halo:
        cp.wait_recv()
    rowi = iota((128, 256), 0)
    coli = iota((128, 256), 1)
    glob = flat * 128 + jnp.where(coli < 192, coli, coli - 256)
    start = jnp.where(
        rowi < 64, jnp.where(rowi < 32, ws[0], ws[1]), jnp.where(rowi < 96, ws[2], ws[3])
    )
    start = jnp.maximum(start, 0)
    stop = jnp.where(
        rowi < 64, jnp.where(rowi < 32, ws[0], ws[1]), jnp.where(rowi < 96, ws[2], ws[3])
    ) + 128
    stop = jnp.minimum(stop, NR * NC * 128)
    valid = jnp.logical_and(glob >= start, glob < stop)
    xf = jnp.concatenate([x_in[...], xh[0], xh[1]], 0).astype(F32)
    x1 = atom_layer(xf, valid, enc_in, enc_out)
    tokrow = (tok[...] - 192 * r).astype(F32)
    tokrows = jnp.broadcast_to(tokrow, (16, 128)).astype(BF16)
    x1all[c, 0:16, :] = tokrows
    x1all[c, 16:144, :] = x1
    x1all[c, 144:160, :] = tokrows

    edge = [
        rcopy(x1all.at[c, 80:160], xe.at[1], e_ss.at[0], e_rs.at[1], nxt),
        rcopy(x1all.at[c, 0:80], xe.at[0], e_ss.at[1], e_rs.at[0], prv),
    ]

    def x1_slot(s):
        return x1all.at[s, 0:144]

    x_send = [
        rcopy(x1_slot(c), x1_slot(c), x_ss.at[j], x_rs.at[c], chip(j)) for j in range(1, NCH)
    ]
    x_fwd = []
    for j in range(NCH):
        s = 2 * ((i + j) % NCH) + k
        x_fwd.append(rcopy(x1_slot(s), x1_slot(s), x_ss.at[NCH + j], x_rs.at[s], sib))
    x_far = []
    for j in range(NCH):
        s = 2 * ((i + j) % NCH) + 1 - k
        x_far.append(rcopy(x1_slot(s), x1_slot(s), x_ss.at[NCH + j], x_rs.at[s], sib))
    for cp in x_send:
        cp.start()
    x_fwd[0].start()
    for cp in edge:
        cp.start()

    for cp in ld_slab:
        cp.wait()
    e_row = iota((256, 256), 0) - shift
    e_col = iota((256, 256), 1)

    def picker(lo, hi, first):
        hit = jnp.logical_and(e_col >= lo, e_col < hi)
        return jnp.logical_and(hit, e_row == e_col - lo + first)

    def onehot(m):
        return jnp.where(m, 1.0, 0.0).astype(BF16)

    pick_q = onehot(picker(0, 96, 0))
    pick_g = onehot(jnp.logical_or(picker(128, 192, 32), picker(224, 256, 0)))
    pick_k = onehot(picker(0, 96, 0))
    pick_v = onehot(picker(96, 192, 0))

    @pl.loop(0, 2)
    def _(m):
        wq[2 * m] = (dot(slab[4 * m], pick_q) + dot(slab[4 * m + 3], pick_g)).astype(BF16)
        wq[2 * m + 1] = (dot(slab[4 * m + 1], pick_k) + dot(slab[4 * m + 2], pick_v)).astype(BF16)

    some_bulk(15 - EARLY)
    for cp in ld_pool:
        cp.wait()
    want = (iota((QT, 128), 0) + QT * k).astype(F32)

    def pool_slot(s, n):
        feats[n] = jnp.maximum(dot(x1all[s, 16:144, :], pool[...]), 0.0).astype(BF16)
        t = x1all[s, 0:16, :].astype(F32)[0:1]
        hots[n] = jnp.where(t == want, 1.0, 0.0).astype(BF16)

    def pool_group(g):
        hot = jnp.concatenate([hots[4 * g + d] for d in range(4)], 1)
        part = dot(hot, feats[4 * g : 4 * g + 4].reshape(512, 768))
        n = hot[:, 0:128].astype(F32)
        for d in range(1, 4):
            n = n + hot[:, 128 * d : 128 * d + 128].astype(F32)
        if g == 0:
            act[...] = part
        else:
            act[...] += part
        return n

    cnt = jnp.zeros((QT, 128), F32)
    for j in range(NCH):
        s = 2 * ((i + j) % NCH) + k
        if j > 0:
            rcopy(x1_slot(s), x1_slot(s), x_ss.at[0], x_rs.at[s], sib).wait_recv()
            x_fwd[j].start()
        pool_slot(s, j)
        if j % 4 == 3:
            cnt = cnt + pool_group(j // 4)
    for j in range(NCH):
        x_far[j].wait_recv()
        pool_slot(2 * ((i + j) % NCH) + 1 - k, NCH + j)
        if j % 4 == 3:
            cnt = cnt + pool_group(2 + j // 4)
    act[...] = act[...] / jnp.sum(cnt, -1, keepdims=True) + cond[...].astype(F32)

    nvalid = jnp.sum(
        jnp.sum(mask[...].astype(F32), 1, keepdims=True), 0, keepdims=True
    )
    lane = iota((1, 128), 1)
    lanef = lane.astype(F32)
    mine = 2 * r + k

    left = jnp.where(lane < 64, 1.0, 0.0).astype(BF16)
    right = jnp.where(lane < 64, 0.0, 1.0).astype(BF16)
    pad = jnp.zeros((32, 128), BF16)
    lq = iota((QT, 128), 1)

    def kv_slot(b, s):
        return kv.at[b, s]

    pend = []
    for b in range(2):
        n = normed(act[...]).astype(BF16)
        own_kv = dot(n, wq[2 * b + 1])
        kv[b, mine, 0] = own_kv[0:48, 0:128].astype(BF16)
        kv[b, mine, 1] = jnp.where(
            lane < 64, own_kv[0:48, 128:256], pltpu.roll(own_kv[48:96, 128:256], 64, 1)
        ).astype(BF16)
        kv[b, mine, 2] = own_kv[48:96, 0:128].astype(BF16)
        for j in range(1, NR):
            cp = rcopy(
                kv_slot(b, mine),
                kv_slot(b, mine),
                kv_ss.at[b, j],
                kv_rs.at[b, mine],
                ((r + j) % NR, c),
            )
            cp.start()
            pend.append(cp)
        fwd = []
        for j in range(NR):
            s = 2 * ((r + j) % NR) + k
            fwd.append(
                rcopy(kv_slot(b, s), kv_slot(b, s), kv_ss.at[b, NR + j], kv_rs.at[b, s], sib)
            )
        fwd[0].start()
        pend += fwd
        qg = dot(n, wq[2 * b])
        q = qg[:, 0:128].astype(BF16).astype(F32)
        gate = jax.nn.sigmoid(qg[:, 128:256])
        qs = jnp.concatenate([jnp.where(lq < 48, q, 0.0), jnp.where(lq < 48, 0.0, q)], 0).astype(
            BF16
        )
        for j in range(1, NR):
            s = 2 * ((r + j) % NR) + k
            rcopy(kv_slot(b, s), kv_slot(b, s), kv_ss.at[b, 0], kv_rs.at[b, s], sib).wait_recv()
            fwd[j].start()
        b_own[b].wait()
        for j in range(1, NC):
            s = (c + j) % NC
            rcopy(bb.at[b, s], bb.at[b, s], b_ss.at[b, 0], b_rs.at[b, s], sib).wait_recv()

        def scores(slots, mx):
            keys = []
            for s in slots:
                keys += [kv[b, s, 0], kv[b, s, 2], pad]
            dots = dot_t(qs, jnp.concatenate(keys, 0)) * (1.0 / math.sqrt(48.0))
            for d, slot in enumerate(slots):
                first = (QT * slot).astype(F32)
                ok = lanef + first < jnp.minimum(nvalid, first + QT)
                parts = []
                for h in range(2):
                    m = bb[b, slot, h]
                    tail = jnp.where(
                        lane < 32,
                        pltpu.roll(m[0:24], 32, 1),
                        jnp.where(
                            lane < 64, pltpu.roll(m[24:48], 64, 1), pltpu.roll(m[48:72], 96, 1)
                        ),
                    )
                    parts += [m, tail]
                sc = dots[:, 128 * d : 128 * d + 128] + jnp.concatenate(parts, 0)
                sc = jnp.where(ok, sc, NEG)
                ssc[slot] = sc
                mx = jnp.maximum(mx, sc)
            return mx

        mx = jnp.full((2 * QT, 128), 2 * NEG, F32)
        if b == 0:
            some_bulk(G0)
        for grp in range(4):
            slots = []
            for j in (2 * grp, 2 * grp + 1):
                s = 2 * ((r + j) % NR) + k
                slots.append(s)
            for j in (2 * grp, 2 * grp + 1):
                s = 2 * ((r + j) % NR) + 1 - k
                slots.append(s)
                rcopy(kv_slot(b, s), kv_slot(b, s), kv_ss.at[b, 0], kv_rs.at[b, s], sib).wait_recv()
            mx = scores(slots, mx)
        top = jnp.max(mx, -1, keepdims=True)

        def value_step(s4, state):
            tot, o = state
            ps = []
            vals = []
            for d in range(4):
                s = 4 * s4 + d
                e = jnp.exp(ssc[s] - top)
                tot = tot + e
                ps.append(e.astype(BF16))
                mid = kv[b, s, 1]
                vals.append(jnp.concatenate([kv[b, s, 0], mid * left], 1))
                vals.append(jnp.concatenate([kv[b, s, 2], mid * right], 1))
                vals.append(jnp.concatenate([pad, pad], 1))
            return tot, o + dot(jnp.concatenate(ps, 1), jnp.concatenate(vals, 0))

        tot, o = lax.fori_loop(
            0, 4, value_step, (jnp.zeros((2 * QT, 128), F32), jnp.zeros((2 * QT, 256), F32))
        )
        inv = 1.0 / jnp.sum(tot, -1, keepdims=True)
        o_a = o[:QT, 0:128] * inv[:QT]
        o_b = (o[:, 128:256] + pltpu.roll(o[:, 128:256], 64, 1)) * inv
        o = jnp.where(lq < 16, o_b[:QT], jnp.where(lq < 64, o_b[QT:], jnp.where(lq < 96, 0.0, o_a)))
        ob[b, i] = (gate * o).astype(BF16)
        for j in range(1, NCH):
            cp = rcopy(ob.at[b, i], ob.at[b, i], o_ss.at[b, j], o_rs.at[b, i], chip(j))
            cp.start()
            pend.append(cp)
        if b == 0:
            some_bulk(G1)
            for cp in ld_tok:
                cp.wait()
            for cp in swap:
                cp.wait_recv()
        for j in range(1, NCH):
            s = (i + j) % NCH
            rcopy(ob.at[b, s], ob.at[b, s], o_ss.at[b, 0], o_rs.at[b, s], sib).wait_recv()
        gated = jnp.concatenate([ob[b, s] for s in range(NCH)], 1)
        act[...] += dot(gated, topad[8 * b : 8 * b + 8].reshape(1024, 768))

        m = normed(act[...]).astype(BF16)
        swish = jax.nn.silu(dot_t(m, tin[b, 0]))
        hidden = (swish * dot_t(m, tin[b, 1])).astype(BF16)
        prt[b] = dot(hidden, tout[b]).astype(BF16)
        for o_ in range(OWN):

            @pl.when(i != o_)
            def _():
                rcopy(
                    prt.at[b, 16 * o_ : 16 * o_ + 16],
                    rsb.at[b, i],
                    r_ss.at[b, o_],
                    r_rs.at[b, i],
                    (r, 2 * o_ + k),
                ).start()

        if b == 0:
            some_bulk(G2)

        @pl.when(is_owner)
        def _():
            row0 = pl.multiple_of(16 * i, 16)
            rsb[b, i] = prt[b, pl.ds(row0, 16), :]
            for j in range(1, NCH):
                s = (i + j) % NCH
                rcopy(rsb.at[b, s], rsb.at[b, s], r_ss.at[b, 0], r_rs.at[b, s], sib).wait_recv()
            total = rsb[b, 0].astype(F32)
            for s in range(1, NCH):
                total = total + rsb[b, s].astype(F32)
            if b == 0:
                db[i] = total.astype(BF16)
                for j in range(1, NCH):
                    rcopy(db.at[i], db.at[i], d_ss.at[j], d_rs.at[i], chip(j)).start()
            else:
                last = act[pl.ds(row0, 16), :] + total
                here = pl.multiple_of(64 + QT * k + 16 * i, 16)
                mine_p = proj.at[pl.ds(here, 16)]
                proj[pl.ds(here, 16), :] = dot(
                    normed(last).astype(BF16), tok_atom[...]
                ).astype(BF16)
                for j in range(1, NC):
                    rcopy(
                        mine_p, mine_p, p_ss.at[j], p_rs.at[OWN * k + i], (r, (c + j) % NC)
                    ).start()

                @pl.when(is_tail)
                def _():
                    rcopy(
                        mine_p,
                        proj.at[pl.ds(pl.multiple_of(16 * (i - 2), 16), 16)],
                        p_ss.at[16],
                        p_rs.at[10 + i],
                        ((r + 1) % NR, 0),
                    ).start()

                @pl.when(is_head)
                def _():
                    rcopy(
                        mine_p,
                        proj.at[pl.ds(pl.multiple_of(256 + 16 * i, 16), 16)],
                        p_ss.at[16],
                        p_rs.at[12 + i],
                        ((r + NR - 1) % NR, NC - 1),
                    ).start()

        if b == 0:
            some_bulk(15)
            for o_ in range(OWN):

                @pl.when(i != o_)
                def _():
                    rcopy(db.at[o_], db.at[o_], d_ss.at[0], d_rs.at[o_], sib).wait_recv()

            act[...] += jnp.concatenate([db[s].astype(F32) for s in range(OWN)], 0)

    for cp in edge:
        cp.wait_recv()
    half = iota((1, 128), 1) < 64
    high = xe[0, 0:16, :].astype(F32)[0:1] + jnp.where(c == NC - 1, 192.0, 0.0)
    low = xe[1, 64:80, :].astype(F32)[0:1] - jnp.where(c == 0, 192.0, 0.0)
    side = jnp.where(half, high, low) + 64.0
    tcol = jnp.concatenate(
        [
            jnp.transpose(jnp.broadcast_to(tokrow + 64.0, (128, 128))),
            jnp.transpose(jnp.broadcast_to(side, (128, 128))),
        ],
        0,
    )
    lane2 = iota((256, 128), 1).astype(F32)
    hot = jnp.concatenate(
        [jnp.where(tcol == lane2 + 128.0 * t, 1.0, 0.0) for t in range(3)], 1
    ).astype(BF16)
    x1cat = jnp.concatenate([x1all[c, 16:144, :], xe[0, 16:80, :], xe[1, 0:64, :]], 0).astype(F32)

    def proj_wait(slot, row, n):
        ref = proj.at[row : row + n]
        rcopy(ref, ref, p_ss.at[0], p_rs.at[slot], sib).wait_recv()

    for s in range(2 * OWN):

        @pl.when(jnp.logical_or(i >= OWN, s != OWN * k + i))
        def _():
            proj_wait(s, 64 + 16 * s, 16)

    @pl.when(c == 0)
    def _():
        for s in range(4):
            proj_wait(12 + s, 16 * s, 16)

    @pl.when(c == NC - 1)
    def _():
        for s in range(4):
            proj_wait(12 + s, 256 + 16 * s, 16)

    spread = dot(hot, proj[...])
    x2 = (x1cat + spread).astype(BF16).astype(F32)
    x3 = atom_layer(x2, valid, dec_in, dec_out)
    n3 = normed(x3.astype(F32)).astype(BF16)
    out[...] = dot_t(pos[...], n3)

    for cp in halo + swap + edge + x_send + x_fwd + b_send[0] + b_send[1] + pend:
        cp.wait_send()
    for b in range(2):
        for o_ in range(OWN):

            @pl.when(i != o_)
            def _():
                src = prt.at[b, 16 * o_ : 16 * o_ + 16]
                rcopy(src, rsb.at[b, i], r_ss.at[b, o_], r_rs.at[b, i], sib).wait_send()

    @pl.when(is_owner)
    def _():
        for j in range(1, NCH):
            rcopy(db.at[i], db.at[i], d_ss.at[j], d_rs.at[i], sib).wait_send()
        ref = proj.at[pl.ds(pl.multiple_of(64 + QT * k + 16 * i, 16), 16)]
        for j in range(1, NC):
            rcopy(ref, ref, p_ss.at[j], p_rs.at[0], sib).wait_send()

        @pl.when(jnp.logical_or(is_tail, is_head))
        def _():
            rcopy(ref, ref, p_ss.at[16], p_rs.at[0], sib).wait_send()


def body(
    atom_feat,
    atom_token,
    window_start,
    token_cond,
    token_mask,
    pair,
    enc_in,
    enc_out,
    pool_weight,
    tok_in,
    tok_out,
    pair_weight,
    trans_in,
    trans_out,
    tok_atom,
    dec_in,
    dec_out,
    pos_out,
):
    vm = pl.BlockSpec(memory_space=pltpu.VMEM)
    hb = pl.BlockSpec(memory_space=pl.ANY)
    dma = pltpu.SemaphoreType.DMA
    wt = jnp.transpose(pair_weight, (0, 2, 1)).reshape(32, 128)
    V = pltpu.VMEM
    scratch = [
        V((QT, 768), BF16),
        V((192, 96, 128), BF16),
        V((4, 128, 128), BF16),
        V((128, 128), BF16),
        V((128, 768), BF16),
        V((8, 768, 256), BF16),
        V((4, 768, 256), BF16),
        V((16, 128, 768), BF16),
        V((2, 2, 192, 768), BF16),
        V((2, 192, 768), BF16),
        V((768, 128), BF16),
        V((4, 128, 128), BF16),
        V((128, 128), BF16),
        V((3, 128), BF16),
        V((2, 64, 128), BF16),
        V((16, 160, 128), BF16),
        V((2, 80, 128), BF16),
        V((32, 144, 128), F32),
        V((2, 16, 2, 72, 128), F32),
        V((2, 16, 3, 48, 128), BF16),
        V((16, 192, 128), F32),
        V((2, 8, QT, 128), BF16),
        V((2, QT, 768), BF16),
        V((2, 8, 16, 768), BF16),
        V((6, 16, 768), BF16),
        V((QT, 768), F32),
        V((16, 128, 768), BF16),
        V((16, QT, 128), BF16),
        V((384, 128), BF16),
        dma((24,)),
        dma((2,)),
        dma((2,)),
        dma((16,)),
        dma((16,)),
        dma((2,)),
        dma((2,)),
        dma((2,)),
        dma((2,)),
        dma((2, 16)),
        dma((2, 16)),
        dma((2, 16)),
        dma((2, 16)),
        dma((2, 8)),
        dma((2, 8)),
        dma((2, 8)),
        dma((2, 8)),
        dma((8,)),
        dma((8,)),
        dma((17,)),
        dma((16,)),
    ]
    return pl.pallas_call(
        kernel,
        out_shape=jax.ShapeDtypeStruct((3, 128), F32),
        in_specs=[pl.BlockSpec(memory_space=pltpu.SMEM)] + [vm] * 4 + [hb] * 13,
        out_specs=vm,
        scratch_shapes=scratch,
        compiler_params=pltpu.CompilerParams(
            collective_id=0, has_side_effects=True, vmem_limit_bytes=56 << 20
        ),
        name="diffusion_step",
    )(
        window_start,
        atom_token.reshape(1, 128),
        token_mask.reshape(12, 128),
        atom_feat,
        wt,
        token_cond,
        pair,
        enc_in,
        enc_out,
        pool_weight,
        tok_in.reshape(8, 768, 768),
        tok_out.reshape(16, 96, 768),
        jnp.swapaxes(trans_in, 2, 3),
        trans_out,
        tok_atom,
        dec_in,
        dec_out,
        pos_out,
    )


def solution(mesh):
    in_specs = (
        P(("row", "col"), None),
        P(("row", "col")),
        P(("row", "col")),
        P("row", None),
        P(),
        P("row", "col", None),
        P(),
        P(),
        P(),
        P(),
        P(),
        P(),
        P(None, None, None, "col"),
        P(None, "col", None),
        P(),
        P(),
        P(),
        P(),
    )
    out_specs = P(None, ("row", "col"))
    return jax.shard_map(body, mesh=mesh, in_specs=in_specs, out_specs=out_specs, check_vma=False)
```

```python
import math

import jax
import jax.numpy as jnp
from jax import lax
from jax.experimental import pallas as pl
from jax.experimental.pallas import tpu as pltpu
from jax.sharding import PartitionSpec as P

MESH = pl.DeviceIdType.MESH
F32 = jnp.float32
BF16 = jnp.bfloat16
NEG = -1000000000.0
NR = 8
NC = 16
NCH = 8
FAR_FIRST = (5, 3, 4, 1, 7, 2, 6)
OWN = 6
CHIP_OF = (0, 3, 6, 5, 2, 1)
QT = 96
BULK = (
    ((0, 2, 0), (0, 6, 0), (0, 4, 0), (0, 1, 0), (0, 7, 0), (0, 3, 0)),
    (),
    ((0, 5, 0), (0, 2, 1), (0, 6, 1), (0, 4, 1), (0, 1, 1), (0, 7, 1), (0, 3, 1), (0, 5, 1), (0, 0, 0)),
    ((1, 2, 0), (1, 6, 0), (1, 4, 0)),
    ((1, 1, 0), (1, 1, 1), (1, 4, 1)),
    ((1, 7, 0), (1, 7, 1)),
    ((1, 3, 0), (1, 3, 1)),
    ((1, 5, 0), (1, 5, 1)),
    ((1, 2, 1), (1, 6, 1), (1, 0, 0)),
)
ZR = 80
BT = 8


def dot(a, b):
    return jnp.dot(a, b, preferred_element_type=F32)


def dot_t(a, b):
    return lax.dot_general(a, b, (((1,), (1,)), ((), ())), preferred_element_type=F32)


def normed(x):
    cent = x - jnp.mean(x, -1, keepdims=True)
    var = jnp.mean(cent * cent, -1, keepdims=True)
    return cent * lax.rsqrt(var + 1e-05)


def iota(shape, dim):
    return lax.broadcasted_iota(jnp.int32, shape, dim)


def atom_layer(xf, valid, w_in, w_out):
    n = normed(xf).astype(BF16)
    own = n[:128]
    q = dot(own, w_in[0]).astype(BF16).astype(F32)
    keys = dot(n, w_in[1]).astype(BF16)
    vals = dot(n, w_in[2]).astype(BF16)
    gate = dot(own, w_in[3])
    head = iota((128, 128), 1) // 32
    outs = jnp.zeros((128, 128), F32)
    for h in range(4):
        qh = jnp.where(head == h, q, 0.0).astype(BF16)
        s = dot_t(qh, keys) * (1.0 / math.sqrt(32.0))
        s = jnp.where(valid, s, NEG)
        e = jnp.exp(s - jnp.max(s, -1, keepdims=True))
        total = jnp.sum(e, -1, keepdims=True)
        o = dot(e.astype(BF16), vals) / total
        outs = jnp.where(head == h, o, outs)
    gated = (jax.nn.sigmoid(gate) * outs).astype(BF16)
    return (xf[:128] + dot(gated, w_out[...])).astype(BF16)


def kernel(
    ws,
    tok,
    mask,
    x_in,
    wt,
    cond_h,
    pair_h,
    enc_in_h,
    enc_out_h,
    pool_h,
    tok_in_h,
    tok_out_h,
    tin_h,
    tout_h,
    tok_atom_h,
    dec_in_h,
    dec_out_h,
    pos_h,
    out,
    cond,
    pair,
    enc_in,
    enc_out,
    pool,
    slab,
    wq,
    topad,
    tin,
    tout,
    tok_atom,
    dec_in,
    dec_out,
    pos,
    xh,
    x1all,
    xe,
    zb,
    bb,
    kv,
    ssc,
    vb,
    ob,
    prt,
    rsb,
    db,
    act,
    feats,
    hots,
    proj,
    lsem,
    h_ss,
    h_rs,
    x_ss,
    x_rs,
    e_ss,
    e_rs,
    t_ss,
    t_rs,
    b_ss,
    b_rs,
    kv_ss,
    kv_rs,
    o_ss,
    o_rs,
    r_ss,
    r_rs,
    d_ss,
    d_rs,
    p_ss,
    p_rs,
):
    r = lax.axis_index("row")
    c = lax.axis_index("col")
    i = c // 2
    k = c % 2
    sib = (r, c + 1 - 2 * k)
    flat = r * NC + c
    nxt = (flat + 1) % (NR * NC)
    prv = (flat + NR * NC - 1) % (NR * NC)
    nxt = (nxt // NC, nxt % NC)
    prv = (prv // NC, prv % NC)
    turned = (i + 4 * k) % NCH
    unit = OWN + 0 * i
    for u in range(OWN):
        unit = jnp.where(turned == CHIP_OF[u], u, unit)
    is_owner = unit < OWN
    is_tail = jnp.logical_and(k == 1, jnp.logical_and(unit >= 2, is_owner))
    is_head = jnp.logical_and(k == 0, unit < 4)

    def owner_dev(u):
        return (r, 2 * ((CHIP_OF[u] + 4 * k) % NCH) + k)


    def chip(j):
        return (r, 2 * ((i + j) % NCH) + k)

    def rcopy(src, dst, ss, rs, dev):
        return pltpu.make_async_remote_copy(
            src_ref=src, dst_ref=dst, send_sem=ss, recv_sem=rs, device_id=dev, device_id_type=MESH
        )

    nload = [0]

    def load(src, dst):
        cp = pltpu.make_async_copy(src, dst, lsem.at[nload[0]])
        nload[0] += 1
        cp.start()
        return cp

    ld_pair = [load(pair_h.at[48 * j : 48 * j + 48], pair.at[48 * j : 48 * j + 48]) for j in range(4)]
    ld_enc = [load(enc_in_h, enc_in), load(enc_out_h, enc_out)]
    ld_pool = [
        load(pool_h, pool),
        load(cond_h.at[pl.ds(pl.multiple_of(QT * k, 32), QT)], cond),
    ]
    base = jnp.minimum(128 * ((QT * i) // 128), 512)
    base = pl.multiple_of(base, 128)
    shift = QT * i - base
    ld_slab = [load(tok_in_h.at[:, :, pl.ds(base, 256)], slab)]
    core_rows = pl.ds(pl.multiple_of(QT * k, 32), QT)
    tin_k = tin.at[:, :, core_rows, :]
    tout_k = tout.at[:, core_rows, :]
    ld_tok = [
        load(tok_out_h.at[:, 32:96], topad.at[:, 0:64]),
        load(tok_out_h.at[:, 0:32], topad.at[:, 96:128]),
        load(tin_h, tin_k),
        load(tout_h, tout_k),
        load(tok_atom_h, tok_atom),
        load(dec_in_h, dec_in),
        load(dec_out_h, dec_out),
        load(pos_h, pos),
    ]

    zb[:, :, 72:, :] = jnp.zeros((16, 2, 8, 128), jnp.int32)
    vb[:, 96:128, :] = jnp.zeros((16, 32, 256), BF16)
    topad[:, 64:96, :] = jnp.zeros((16, 32, 768), BF16)
    proj[...] = jnp.zeros((384, 128), BF16)

    order = iota((32, 32), 1) == 16 * (iota((32, 32), 0) // 16) + 2 * (iota((32, 32), 0) % 8) + (
        iota((32, 32), 0) // 8
    ) % 2
    w_heads = dot(jnp.where(order, 1.0, 0.0).astype(BF16), wt[...]).astype(BF16)
    lane32 = iota((32, 128), 1)
    zf = zb.reshape(16 * 2 * ZR, 128)

    def bias_half(kp):
        def words(u, first):
            return lax.shift_left(u[first : first + 8], 16) | u[first + 8 : first + 16]

        def put(b, row, value):
            zf[pl.ds(b * 16 * ZR + kp * ZR + row, 8, stride=2 * ZR), :] = value

        sizes = jnp.zeros((32, 128), jnp.int32)
        for kb in range(3):

            def tiles(n, sizes):
                t = 24 * kb + BT * n
                rows = []
                for d in range(BT):
                    rows.append(pair[QT * kp + t + d])
                    rows.append(pair[QT * kp + 72 + BT * n + d, 32 * kb : 32 * kb + 32, :])
                res = dot_t(w_heads, jnp.concatenate(rows, 0))
                for d in range(BT):
                    x = res[:, 128 * d : 128 * d + 128]
                    most = jnp.max(jnp.abs(x), -1, keepdims=True)
                    size = (most * (65536.0 * 1.000001)).astype(jnp.int32) + 1
                    sizes = sizes + jnp.where(lane32 == t + d, size, 0)
                    inv = (32767.0 * 65536.0) / size.astype(F32)
                    u = (x * inv + 32768.5).astype(jnp.int32)
                    for b in range(2):
                        put(b, t + d, words(u, 16 * b))
                return sizes

            sizes = lax.fori_loop(0, 24 // BT, tiles, sizes)
        for b in range(2):
            for odd in range(2):
                put(b, 72 + odd, sizes[16 * b + 8 * odd : 16 * b + 8 * odd + 8])

    bar = pltpu.get_barrier_semaphore()

    def greet(dev):
        pl.semaphore_signal(bar, inc=1, device_id=dev, device_id_type=MESH)

    for j in range(1, NC):
        greet((r, (c + j) % NC))
    for j in range(1, NR):
        greet(((r + j) % NR, c))
    greet(nxt)
    greet(prv)

    @pl.when(c == 0)
    def _():
        for u in range(2, OWN):
            greet(((r + NR - 1) % NR, 2 * ((CHIP_OF[u] + 4) % NCH) + 1))

    @pl.when(c == NC - 1)
    def _():
        for u in range(4):
            greet(((r + 1) % NR, 2 * CHIP_OF[u]))

    ld_pair[0].wait()
    ld_pair[1].wait()
    bias_half(0)
    extra = jnp.where(jnp.logical_or(is_tail, is_head), 1, 0)
    pl.semaphore_wait(bar, 24 + extra)

    halo = [
        rcopy(x_in.at[64:128], xh.at[1], h_ss.at[0], h_rs.at[1], nxt),
        rcopy(x_in.at[0:64], xh.at[0], h_ss.at[1], h_rs.at[0], prv),
    ]
    for cp in halo:
        cp.start()
    swap = [
        rcopy(tin_h, tin_k, t_ss.at[0], t_rs.at[0], sib),
        rcopy(tout_h, tout_k, t_ss.at[1], t_rs.at[1], sib),
    ]
    for cp in swap:
        cp.start()

    def bias_src(b, ch, core):
        return zb.at[8 * b + ch, core]

    def bias_send(b, j, core):
        ch = (i + j) % NCH
        return rcopy(
            bias_src(b, ch, core), bb.at[b, c], b_ss.at[b, 2 * j + core], b_rs.at[b, c], (r, 2 * ch + core)
        )

    def bias_sib(b):
        return rcopy(bias_src(b, i, 1 - k), bb.at[b, c], b_ss.at[b, 0], b_rs.at[b, c], sib)

    b_sent = []

    def some_bulk(when):
        for b, j, core in BULK[when]:
            b_sent.append(bias_sib(b) if j == 0 else bias_send(b, j, core))
            b_sent[-1].start()

    some_bulk(0)
    ld_pair[2].wait()
    ld_pair[3].wait()
    bias_half(1)
    b_own = []
    for b in range(2):
        cp = pltpu.make_async_copy(bias_src(b, i, k), bb.at[b, c], lsem.at[nload[0] + b])
        cp.start()
        b_own.append(cp)

    some_bulk(1)
    for cp in ld_enc:
        cp.wait()
    for cp in halo:
        cp.wait_recv()
    rowi = iota((128, 256), 0)
    coli = iota((128, 256), 1)
    glob = flat * 128 + jnp.where(coli < 192, coli, coli - 256)
    start = jnp.where(
        rowi < 64, jnp.where(rowi < 32, ws[0], ws[1]), jnp.where(rowi < 96, ws[2], ws[3])
    )
    start = jnp.maximum(start, 0)
    stop = jnp.where(
        rowi < 64, jnp.where(rowi < 32, ws[0], ws[1]), jnp.where(rowi < 96, ws[2], ws[3])
    ) + 128
    stop = jnp.minimum(stop, NR * NC * 128)
    valid = jnp.logical_and(glob >= start, glob < stop)
    xf = jnp.concatenate([x_in[...], xh[0], xh[1]], 0).astype(F32)
    x1 = atom_layer(xf, valid, enc_in, enc_out)
    tokrow = (tok[...] - 192 * r).astype(F32)
    tokrows = jnp.broadcast_to(tokrow, (16, 128)).astype(BF16)
    x1all[c, 0:16, :] = tokrows
    x1all[c, 16:144, :] = x1
    x1all[c, 144:160, :] = tokrows

    edge = [
        rcopy(x1all.at[c, 80:160], xe.at[1], e_ss.at[0], e_rs.at[1], nxt),
        rcopy(x1all.at[c, 0:80], xe.at[0], e_ss.at[1], e_rs.at[0], prv),
    ]

    def x1_slot(s):
        return x1all.at[s, 0:144]

    x_send = [
        rcopy(x1_slot(c), x1_slot(c), x_ss.at[j], x_rs.at[c], chip(j)) for j in FAR_FIRST
    ]
    x_fwd = []
    for j in range(NCH):
        s = 2 * ((i + j) % NCH) + k
        x_fwd.append(rcopy(x1_slot(s), x1_slot(s), x_ss.at[NCH + j], x_rs.at[s], sib))
    x_far = []
    for j in range(NCH):
        s = 2 * ((i + j) % NCH) + 1 - k
        x_far.append(rcopy(x1_slot(s), x1_slot(s), x_ss.at[NCH + j], x_rs.at[s], sib))
    for cp in x_send:
        cp.start()
    x_fwd[0].start()
    for cp in edge:
        cp.start()

    for cp in ld_slab:
        cp.wait()
    e_row = iota((256, 256), 0) - shift
    e_col = iota((256, 256), 1)

    def picker(lo, hi, first):
        hit = jnp.logical_and(e_col >= lo, e_col < hi)
        return jnp.logical_and(hit, e_row == e_col - lo + first)

    def onehot(m):
        return jnp.where(m, 1.0, 0.0).astype(BF16)

    pick_q = onehot(picker(0, 96, 0))
    pick_g = onehot(jnp.logical_or(picker(128, 192, 32), picker(224, 256, 0)))
    pick_k = onehot(picker(0, 96, 0))
    pick_v = onehot(picker(96, 192, 0))

    @pl.loop(0, 2)
    def _(m):
        wq[2 * m] = (dot(slab[4 * m], pick_q) + dot(slab[4 * m + 3], pick_g)).astype(BF16)
        wq[2 * m + 1] = (dot(slab[4 * m + 1], pick_k) + dot(slab[4 * m + 2], pick_v)).astype(BF16)

    some_bulk(2)
    for cp in ld_pool:
        cp.wait()
    want = (iota((QT, 128), 0) + QT * k).astype(F32)

    def pool_slot(s, n):
        feats[n] = jnp.maximum(dot(x1all[s, 16:144, :], pool[...]), 0.0).astype(BF16)
        t = x1all[s, 0:16, :].astype(F32)[0:1]
        hots[n] = jnp.where(t == want, 1.0, 0.0).astype(BF16)

    def pool_group(g):
        hot = jnp.concatenate([hots[4 * g + d] for d in range(4)], 1)
        part = dot(hot, feats[4 * g : 4 * g + 4].reshape(512, 768))
        n = hot[:, 0:128].astype(F32)
        for d in range(1, 4):
            n = n + hot[:, 128 * d : 128 * d + 128].astype(F32)
        if g == 0:
            act[...] = part
        else:
            act[...] += part
        return n

    cnt = jnp.zeros((QT, 128), F32)
    for j in range(NCH):
        s = 2 * ((i + j) % NCH) + k
        if j > 0:
            rcopy(x1_slot(s), x1_slot(s), x_ss.at[0], x_rs.at[s], sib).wait_recv()
            x_fwd[j].start()
        pool_slot(s, j)
        if j % 4 == 3:
            cnt = cnt + pool_group(j // 4)
    for j in range(NCH):
        x_far[j].wait_recv()
        pool_slot(2 * ((i + j) % NCH) + 1 - k, NCH + j)
        if j % 4 == 3:
            cnt = cnt + pool_group(2 + j // 4)
    act[...] = act[...] / jnp.sum(cnt, -1, keepdims=True) + cond[...].astype(F32)

    nvalid = jnp.sum(
        jnp.sum(mask[...].astype(F32), 1, keepdims=True), 0, keepdims=True
    )
    lane = iota((1, 128), 1)
    lanef = lane.astype(F32)
    mine = 2 * r + k

    left = jnp.where(lane < 64, 1.0, 0.0).astype(BF16)
    right = jnp.where(lane < 64, 0.0, 1.0).astype(BF16)
    pad = jnp.zeros((32, 128), BF16)
    lq = iota((QT, 128), 1)

    def kv_slot(b, s):
        return kv.at[b, s]

    pend = []
    for b in range(2):
        n = normed(act[...]).astype(BF16)
        own_kv = dot(n, wq[2 * b + 1])
        kv[b, mine, 0] = own_kv[0:48, 0:128].astype(BF16)
        kv[b, mine, 1] = jnp.where(
            lane < 64, own_kv[0:48, 128:256], pltpu.roll(own_kv[48:96, 128:256], 64, 1)
        ).astype(BF16)
        kv[b, mine, 2] = own_kv[48:96, 0:128].astype(BF16)
        for j in FAR_FIRST:
            cp = rcopy(
                kv_slot(b, mine),
                kv_slot(b, mine),
                kv_ss.at[b, j],
                kv_rs.at[b, mine],
                ((r + j) % NR, c),
            )
            cp.start()
            pend.append(cp)
        fwd = []
        for j in range(NR):
            s = 2 * ((r + j) % NR) + k
            fwd.append(
                rcopy(kv_slot(b, s), kv_slot(b, s), kv_ss.at[b, NR + j], kv_rs.at[b, s], sib)
            )
        fwd[0].start()
        pend += fwd
        some_bulk(3 if b == 0 else 8)
        qg = dot(n, wq[2 * b])
        q = qg[:, 0:128].astype(BF16).astype(F32)
        gate = jax.nn.sigmoid(qg[:, 128:256])
        qs = jnp.concatenate([jnp.where(lq < 48, q, 0.0), jnp.where(lq < 48, 0.0, q)], 0).astype(
            BF16
        )
        for j in reversed(FAR_FIRST):
            s = 2 * ((r + j) % NR) + k
            rcopy(kv_slot(b, s), kv_slot(b, s), kv_ss.at[b, 0], kv_rs.at[b, s], sib).wait_recv()
            fwd[j].start()
        b_own[b].wait()
        for j in range(1, NC):
            s = (c + j) % NC
            rcopy(bb.at[b, s], bb.at[b, s], b_ss.at[b, 0], b_rs.at[b, s], sib).wait_recv()

        sizes = jnp.concatenate([bb[b, s, 72:ZR, :] for s in range(NC)], 0).astype(F32)
        steps = jnp.transpose(sizes * (1.0 / (32767.0 * 65536.0)))

        def scores(slots, mx):
            keys = []
            for s in slots:
                keys += [kv[b, s, 0], kv[b, s, 2], pad]
            dots = dot_t(qs, jnp.concatenate(keys, 0)) * (1.0 / math.sqrt(48.0))
            for d, slot in enumerate(slots):
                ok = lanef + QT * slot < jnp.minimum(nvalid, QT * slot + QT)
                word = bb[b, slot, 0:72, :]
                both = (lax.shift_right_logical(word, 16), word & 65535)
                parts = []
                for h in range(2):
                    step = steps[0:72, 8 * slot + h : 8 * slot + h + 1]
                    m = (both[h].astype(F32) - 32768.0) * step
                    tail = jnp.where(
                        lane < 32,
                        pltpu.roll(m[0:24], 32, 1),
                        jnp.where(
                            lane < 64, pltpu.roll(m[24:48], 64, 1), pltpu.roll(m[48:72], 96, 1)
                        ),
                    )
                    parts += [m, tail]
                sc = dots[:, 128 * d : 128 * d + 128] + jnp.concatenate(parts, 0)
                sc = jnp.where(ok, sc, NEG)
                ssc[slot] = sc
                mid = kv[b, slot, 1]
                vb[slot, 0:48, 0:128] = kv[b, slot, 0]
                vb[slot, 0:48, 128:256] = mid * left
                vb[slot, 48:96, 0:128] = kv[b, slot, 2]
                vb[slot, 48:96, 128:256] = mid * right
                mx = jnp.maximum(mx, sc)
            return mx

        mx = jnp.full((2 * QT, 128), 2 * NEG, F32)
        if b == 0:
            some_bulk(4)
        for grp in range(4):
            for row in (2 * grp, 2 * grp + 1):
                s = 2 * row + 1 - k
                rcopy(kv_slot(b, s), kv_slot(b, s), kv_ss.at[b, 0], kv_rs.at[b, s], sib).wait_recv()
            slots = [4 * grp + d for d in range(4)]
            mx = scores(slots, mx)
        top = jnp.max(mx, -1, keepdims=True)
        tot = jnp.zeros((2 * QT, 128), F32)
        ps = []
        for s in range(NC):
            e = jnp.exp(ssc[s] - top)
            tot = tot + e
            ps.append(e.astype(BF16))
        o = dot(jnp.concatenate(ps, 1), vb[...].reshape(NC * 128, 256))
        inv = 1.0 / jnp.sum(tot, -1, keepdims=True)
        o_a = o[:QT, 0:128] * inv[:QT]
        o_b = (o[:, 128:256] + pltpu.roll(o[:, 128:256], 64, 1)) * inv
        o = jnp.where(lq < 16, o_b[:QT], jnp.where(lq < 64, o_b[QT:], jnp.where(lq < 96, 0.0, o_a)))
        ob[b, i] = (gate * o).astype(BF16)
        for j in FAR_FIRST:
            cp = rcopy(ob.at[b, i], ob.at[b, i], o_ss.at[b, j], o_rs.at[b, i], chip(j))
            cp.start()
            pend.append(cp)
        if b == 0:
            some_bulk(5)
            for cp in ld_tok:
                cp.wait()
            for cp in swap:
                cp.wait_recv()
        for j in range(1, NCH):
            s = (i + j) % NCH
            rcopy(ob.at[b, s], ob.at[b, s], o_ss.at[b, 0], o_rs.at[b, s], sib).wait_recv()
        gated = jnp.concatenate([ob[b, s] for s in range(NCH)], 1)
        mid_act = act[...] + dot(gated, topad[8 * b : 8 * b + 8].reshape(1024, 768))
        act[...] = mid_act

        m = normed(mid_act).astype(BF16)
        swish = jax.nn.silu(dot_t(m, tin[b, 0]))
        hidden = (swish * dot_t(m, tin[b, 1])).astype(BF16)
        prt[b] = dot(hidden, tout[b]).astype(BF16)
        for u in range(OWN):

            @pl.when(unit != u)
            def _():
                rcopy(
                    prt.at[b, 16 * u : 16 * u + 16],
                    rsb.at[b, i],
                    r_ss.at[b, u],
                    r_rs.at[b, i],
                    owner_dev(u),
                ).start()

        if b == 0:
            some_bulk(6)

        @pl.when(is_owner)
        def _():
            row0 = pl.multiple_of(16 * unit, 16)
            rsb[b, i] = prt[b, pl.ds(row0, 16), :]
            for j in range(1, NCH):
                s = (i + j) % NCH
                rcopy(rsb.at[b, s], rsb.at[b, s], r_ss.at[b, 0], r_rs.at[b, s], sib).wait_recv()
            total = rsb[b, 0].astype(F32)
            for s in range(1, NCH):
                total = total + rsb[b, s].astype(F32)
            if b == 0:
                db[unit] = total.astype(BF16)
                for j in FAR_FIRST:
                    rcopy(
                        db.at[unit], db.at[unit], d_ss.at[j], d_rs.at[unit], chip(j)
                    ).start()
            else:
                last = act[pl.ds(row0, 16), :] + total
                here = pl.multiple_of(64 + QT * k + 16 * unit, 16)
                mine_p = proj.at[pl.ds(here, 16)]
                proj[pl.ds(here, 16), :] = dot(
                    normed(last).astype(BF16), tok_atom[...]
                ).astype(BF16)
                for j in range(1, NC):
                    rcopy(
                        mine_p, mine_p, p_ss.at[j], p_rs.at[OWN * k + unit], (r, (c + j) % NC)
                    ).start()

                @pl.when(is_tail)
                def _():
                    rcopy(
                        mine_p,
                        proj.at[pl.ds(pl.multiple_of(16 * (unit - 2), 16), 16)],
                        p_ss.at[16],
                        p_rs.at[10 + unit],
                        ((r + 1) % NR, 0),
                    ).start()

                @pl.when(is_head)
                def _():
                    rcopy(
                        mine_p,
                        proj.at[pl.ds(pl.multiple_of(256 + 16 * unit, 16), 16)],
                        p_ss.at[16],
                        p_rs.at[12 + unit],
                        ((r + NR - 1) % NR, NC - 1),
                    ).start()

        if b == 0:
            some_bulk(7)
            for o_ in range(OWN):

                @pl.when(unit != o_)
                def _():
                    rcopy(db.at[o_], db.at[o_], d_ss.at[0], d_rs.at[o_], sib).wait_recv()

            act[...] += jnp.concatenate([db[s].astype(F32) for s in range(OWN)], 0)

    for cp in edge:
        cp.wait_recv()
    half = iota((1, 128), 1) < 64
    high = xe[0, 0:16, :].astype(F32)[0:1] + jnp.where(c == NC - 1, 192.0, 0.0)
    low = xe[1, 64:80, :].astype(F32)[0:1] - jnp.where(c == 0, 192.0, 0.0)
    side = jnp.where(half, high, low) + 64.0
    tcol = jnp.concatenate(
        [
            jnp.transpose(jnp.broadcast_to(tokrow + 64.0, (128, 128))),
            jnp.transpose(jnp.broadcast_to(side, (128, 128))),
        ],
        0,
    )
    lane2 = iota((256, 128), 1).astype(F32)
    hot = jnp.concatenate(
        [jnp.where(tcol == lane2 + 128.0 * t, 1.0, 0.0) for t in range(3)], 1
    ).astype(BF16)
    x1cat = jnp.concatenate([x1all[c, 16:144, :], xe[0, 16:80, :], xe[1, 0:64, :]], 0).astype(F32)

    def proj_wait(slot, row, n):
        ref = proj.at[row : row + n]
        rcopy(ref, ref, p_ss.at[0], p_rs.at[slot], sib).wait_recv()

    for s in range(2 * OWN):

        @pl.when(jnp.logical_or(jnp.logical_not(is_owner), s != OWN * k + unit))
        def _():
            proj_wait(s, 64 + 16 * s, 16)

    @pl.when(c == 0)
    def _():
        for s in range(4):
            proj_wait(12 + s, 16 * s, 16)

    @pl.when(c == NC - 1)
    def _():
        for s in range(4):
            proj_wait(12 + s, 256 + 16 * s, 16)

    spread = dot(hot, proj[...])
    x2 = (x1cat + spread).astype(BF16).astype(F32)
    x3 = atom_layer(x2, valid, dec_in, dec_out)
    n3 = normed(x3.astype(F32)).astype(BF16)
    out[...] = dot_t(pos[...], n3)

    for cp in halo + swap + edge + x_send + x_fwd + b_sent + pend:
        cp.wait_send()
    for b in range(2):
        for o_ in range(OWN):

            @pl.when(unit != o_)
            def _():
                src = prt.at[b, 16 * o_ : 16 * o_ + 16]
                rcopy(src, rsb.at[b, i], r_ss.at[b, o_], r_rs.at[b, i], sib).wait_send()

    @pl.when(is_owner)
    def _():
        for j in range(1, NCH):
            rcopy(db.at[0], db.at[0], d_ss.at[j], d_rs.at[0], sib).wait_send()
        ref = proj.at[pl.ds(pl.multiple_of(64 + QT * k + 16 * unit, 16), 16)]
        for j in range(1, NC):
            rcopy(ref, ref, p_ss.at[j], p_rs.at[0], sib).wait_send()

        @pl.when(jnp.logical_or(is_tail, is_head))
        def _():
            rcopy(ref, ref, p_ss.at[16], p_rs.at[0], sib).wait_send()


def body(
    atom_feat,
    atom_token,
    window_start,
    token_cond,
    token_mask,
    pair,
    enc_in,
    enc_out,
    pool_weight,
    tok_in,
    tok_out,
    pair_weight,
    trans_in,
    trans_out,
    tok_atom,
    dec_in,
    dec_out,
    pos_out,
):
    vm = pl.BlockSpec(memory_space=pltpu.VMEM)
    hb = pl.BlockSpec(memory_space=pl.ANY)
    dma = pltpu.SemaphoreType.DMA
    wt = jnp.transpose(pair_weight, (0, 2, 1)).reshape(32, 128)
    V = pltpu.VMEM
    scratch = [
        V((QT, 768), BF16),
        V((192, 96, 128), BF16),
        V((4, 128, 128), BF16),
        V((128, 128), BF16),
        V((128, 768), BF16),
        V((8, 768, 256), BF16),
        V((4, 768, 256), BF16),
        V((16, 128, 768), BF16),
        V((2, 2, 192, 768), BF16),
        V((2, 192, 768), BF16),
        V((768, 128), BF16),
        V((4, 128, 128), BF16),
        V((128, 128), BF16),
        V((3, 128), BF16),
        V((2, 64, 128), BF16),
        V((16, 160, 128), BF16),
        V((2, 80, 128), BF16),
        V((16, 2, ZR, 128), jnp.int32),
        V((2, 16, ZR, 128), jnp.int32),
        V((2, 16, 3, 48, 128), BF16),
        V((16, 192, 128), F32),
        V((16, 128, 256), BF16),
        V((2, 8, QT, 128), BF16),
        V((2, QT, 768), BF16),
        V((2, 8, 16, 768), BF16),
        V((6, 16, 768), BF16),
        V((QT, 768), F32),
        V((16, 128, 768), BF16),
        V((16, QT, 128), BF16),
        V((384, 128), BF16),
        dma((24,)),
        dma((2,)),
        dma((2,)),
        dma((16,)),
        dma((16,)),
        dma((2,)),
        dma((2,)),
        dma((2,)),
        dma((2,)),
        dma((2, 16)),
        dma((2, 16)),
        dma((2, 16)),
        dma((2, 16)),
        dma((2, 8)),
        dma((2, 8)),
        dma((2, 8)),
        dma((2, 8)),
        dma((8,)),
        dma((8,)),
        dma((17,)),
        dma((16,)),
    ]
    return pl.pallas_call(
        kernel,
        out_shape=jax.ShapeDtypeStruct((3, 128), F32),
        in_specs=[pl.BlockSpec(memory_space=pltpu.SMEM)] + [vm] * 4 + [hb] * 13,
        out_specs=vm,
        scratch_shapes=scratch,
        compiler_params=pltpu.CompilerParams(
            collective_id=0, has_side_effects=True, vmem_limit_bytes=56 << 20
        ),
        name="diffusion_step",
    )(
        window_start,
        atom_token.reshape(1, 128),
        token_mask.reshape(12, 128),
        atom_feat,
        wt,
        token_cond,
        pair,
        enc_in,
        enc_out,
        pool_weight,
        tok_in.reshape(8, 768, 768),
        tok_out.reshape(16, 96, 768),
        jnp.swapaxes(trans_in, 2, 3),
        trans_out,
        tok_atom,
        dec_in,
        dec_out,
        pos_out,
    )


def solution(mesh):
    in_specs = (
        P(("row", "col"), None),
        P(("row", "col")),
        P(("row", "col")),
        P("row", None),
        P(),
        P("row", "col", None),
        P(),
        P(),
        P(),
        P(),
        P(),
        P(),
        P(None, None, None, "col"),
        P(None, "col", None),
        P(),
        P(),
        P(),
        P(),
    )
    out_specs = P(None, ("row", "col"))
    return jax.shard_map(body, mesh=mesh, in_specs=in_specs, out_specs=out_specs, check_vma=False)
```

```python
import math

import jax
import jax.numpy as jnp
from jax import lax
from jax.experimental import pallas as pl
from jax.experimental.pallas import tpu as pltpu
from jax.sharding import PartitionSpec as P

MESH = pl.DeviceIdType.MESH
F32 = jnp.float32
BF16 = jnp.bfloat16
NEG = -1000000000.0
NR = 8
NC = 16
NCH = 8
FAR_FIRST = (5, 3, 4, 1, 7, 2, 6)
OWN = 6
CHIP_OF = (0, 3, 6, 5, 2, 1)
QT = 96
BULK = (
    ((0, 2, 0), (0, 6, 0), (0, 4, 0), (0, 1, 0), (0, 7, 0), (0, 3, 0), (0, 5, 0)),
    (),
    ((0, 2, 1), (0, 6, 1), (0, 4, 1), (0, 1, 1), (0, 7, 1), (0, 3, 1), (0, 5, 1), (0, 0, 0)),
    ((1, 2, 0), (1, 6, 0), (1, 4, 0)),
    ((1, 2, 1), (1, 6, 1), (1, 4, 1), (1, 1, 0), (1, 1, 1)),
    ((1, 7, 0), (1, 7, 1)),
    ((1, 3, 0), (1, 3, 1)),
    ((1, 5, 0), (1, 5, 1), (1, 0, 0)),
    (),
)
PRE, POST = (0, 1), (2,)
ZR = 80
BT = 8


def dot(a, b):
    return jnp.dot(a, b, preferred_element_type=F32)


def dot_t(a, b):
    return lax.dot_general(a, b, (((1,), (1,)), ((), ())), preferred_element_type=F32)


def normed(x):
    cent = x - jnp.mean(x, -1, keepdims=True)
    var = jnp.mean(cent * cent, -1, keepdims=True)
    return cent * lax.rsqrt(var + 1e-05)


def iota(shape, dim):
    return lax.broadcasted_iota(jnp.int32, shape, dim)


def atom_layer(xf, valid, w_in, w_out):
    n = normed(xf).astype(BF16)
    own = n[:128]
    q = dot(own, w_in[0]).astype(BF16).astype(F32)
    keys = dot(n, w_in[1]).astype(BF16)
    vals = dot(n, w_in[2]).astype(BF16)
    gate = dot(own, w_in[3])
    head = iota((128, 128), 1) // 32
    outs = jnp.zeros((128, 128), F32)
    for h in range(4):
        qh = jnp.where(head == h, q, 0.0).astype(BF16)
        s = dot_t(qh, keys) * (1.0 / math.sqrt(32.0))
        s = jnp.where(valid, s, NEG)
        e = jnp.exp(s - jnp.max(s, -1, keepdims=True))
        total = jnp.sum(e, -1, keepdims=True)
        o = dot(e.astype(BF16), vals) / total
        outs = jnp.where(head == h, o, outs)
    gated = (jax.nn.sigmoid(gate) * outs).astype(BF16)
    return (xf[:128] + dot(gated, w_out[...])).astype(BF16)


def kernel(
    ws,
    tok,
    mask,
    x_in,
    wt,
    cond_h,
    pair_h,
    enc_in_h,
    enc_out_h,
    pool_h,
    tok_in_h,
    tok_out_h,
    tin_h,
    tout_h,
    tok_atom_h,
    dec_in_h,
    dec_out_h,
    pos_h,
    out,
    cond,
    pair,
    enc_in,
    enc_out,
    pool,
    slab,
    wq,
    topad,
    tin,
    tout,
    tok_atom,
    dec_in,
    dec_out,
    pos,
    xh,
    x1all,
    xe,
    zb,
    bb,
    kv,
    ssc,
    vb,
    ob,
    prt,
    rsb,
    db,
    act,
    proj,
    lsem,
    h_ss,
    h_rs,
    x_ss,
    x_rs,
    e_ss,
    e_rs,
    t_ss,
    t_rs,
    b_ss,
    b_rs,
    kv_ss,
    kv_rs,
    o_ss,
    o_rs,
    r_ss,
    r_rs,
    d_ss,
    d_rs,
    p_ss,
    p_rs,
):
    r = lax.axis_index("row")
    c = lax.axis_index("col")
    i = c // 2
    k = c % 2
    sib = (r, c + 1 - 2 * k)
    flat = r * NC + c
    nxt = (flat + 1) % (NR * NC)
    prv = (flat + NR * NC - 1) % (NR * NC)
    nxt = (nxt // NC, nxt % NC)
    prv = (prv // NC, prv % NC)
    turned = (i + 4 * k) % NCH
    unit = OWN + 0 * i
    for u in range(OWN):
        unit = jnp.where(turned == CHIP_OF[u], u, unit)
    is_owner = unit < OWN
    is_tail = jnp.logical_and(k == 1, jnp.logical_and(unit >= 2, is_owner))
    is_head = jnp.logical_and(k == 0, unit < 4)

    def owner_dev(u):
        return (r, 2 * ((CHIP_OF[u] + 4 * k) % NCH) + k)


    def chip(j):
        return (r, 2 * ((i + j) % NCH) + k)

    def rcopy(src, dst, ss, rs, dev):
        return pltpu.make_async_remote_copy(
            src_ref=src, dst_ref=dst, send_sem=ss, recv_sem=rs, device_id=dev, device_id_type=MESH
        )

    nload = [0]

    def load(src, dst):
        cp = pltpu.make_async_copy(src, dst, lsem.at[nload[0]])
        nload[0] += 1
        cp.start()
        return cp

    ld_pair = [load(pair_h.at[48 * j : 48 * j + 48], pair.at[48 * j : 48 * j + 48]) for j in range(4)]
    ld_enc = [load(enc_in_h, enc_in), load(enc_out_h, enc_out)]
    ld_pool = [
        load(pool_h, pool),
        load(cond_h.at[pl.ds(pl.multiple_of(QT * k, 32), QT)], cond),
    ]
    base = jnp.minimum(128 * ((QT * i) // 128), 512)
    base = pl.multiple_of(base, 128)
    shift = QT * i - base
    ld_slab = [load(tok_in_h.at[:, :, pl.ds(base, 256)], slab)]
    core_rows = pl.ds(pl.multiple_of(QT * k, 32), QT)
    tin_k = tin.at[:, :, core_rows, :]
    tout_k = tout.at[:, core_rows, :]
    ld_tok = [
        load(tok_out_h.at[:, 32:96], topad.at[:, 0:64]),
        load(tok_out_h.at[:, 0:32], topad.at[:, 96:128]),
        load(tin_h, tin_k),
        load(tout_h, tout_k),
        load(tok_atom_h, tok_atom),
        load(dec_in_h, dec_in),
        load(dec_out_h, dec_out),
        load(pos_h, pos),
    ]

    zb[:, :, 72:, :] = jnp.zeros((16, 2, 8, 128), jnp.int32)
    vb[:, 96:128, :] = jnp.zeros((16, 32, 256), BF16)
    topad[:, 64:96, :] = jnp.zeros((16, 32, 768), BF16)
    proj[...] = jnp.zeros((384, 128), BF16)

    order = iota((32, 32), 1) == 16 * (iota((32, 32), 0) // 16) + 2 * (iota((32, 32), 0) % 8) + (
        iota((32, 32), 0) // 8
    ) % 2
    w_heads = dot(jnp.where(order, 1.0, 0.0).astype(BF16), wt[...]).astype(BF16)
    lane32 = iota((32, 128), 1)
    zf = zb.reshape(16 * 2 * ZR, 128)

    def bias_part(kp, parts, sizes):
        def words(u, first):
            return lax.shift_left(u[first : first + 8], 16) | u[first + 8 : first + 16]

        def put(b, row, value):
            zf[pl.ds(b * 16 * ZR + kp * ZR + row, 8, stride=2 * ZR), :] = value

        for kb in parts:

            def tiles(n, sizes):
                t = 24 * kb + BT * n
                rows = []
                for d in range(BT):
                    rows.append(pair[QT * kp + t + d])
                    rows.append(pair[QT * kp + 72 + BT * n + d, 32 * kb : 32 * kb + 32, :])
                res = dot_t(w_heads, jnp.concatenate(rows, 0))
                for d in range(BT):
                    x = res[:, 128 * d : 128 * d + 128]
                    most = jnp.max(jnp.abs(x), -1, keepdims=True)
                    size = (most * (65536.0 * 1.000001)).astype(jnp.int32) + 1
                    sizes = sizes + jnp.where(lane32 == t + d, size, 0)
                    inv = (32767.0 * 65536.0) / size.astype(F32)
                    u = (x * inv + 32768.5).astype(jnp.int32)
                    for b in range(2):
                        put(b, t + d, words(u, 16 * b))
                return sizes

            sizes = lax.fori_loop(0, 24 // BT, tiles, sizes)
        if 2 not in parts:
            return sizes
        for b in range(2):
            for odd in range(2):
                put(b, 72 + odd, sizes[16 * b + 8 * odd : 16 * b + 8 * odd + 8])

    bar = pltpu.get_barrier_semaphore()

    def greet(dev):
        pl.semaphore_signal(bar, inc=1, device_id=dev, device_id_type=MESH)

    for j in range(1, NC):
        greet((r, (c + j) % NC))
    for j in range(1, NR):
        greet(((r + j) % NR, c))
    greet(nxt)
    greet(prv)

    @pl.when(c == 0)
    def _():
        for u in range(2, OWN):
            greet(((r + NR - 1) % NR, 2 * ((CHIP_OF[u] + 4) % NCH) + 1))

    @pl.when(c == NC - 1)
    def _():
        for u in range(4):
            greet(((r + 1) % NR, 2 * CHIP_OF[u]))

    ld_pair[0].wait()
    ld_pair[1].wait()
    no_sizes = jnp.zeros((32, 128), jnp.int32)
    sizes = bias_part(0, PRE, no_sizes)
    extra = jnp.where(jnp.logical_or(is_tail, is_head), 1, 0)
    pl.semaphore_wait(bar, 24 + extra)

    halo = [
        rcopy(x_in.at[64:128], xh.at[1], h_ss.at[0], h_rs.at[1], nxt),
        rcopy(x_in.at[0:64], xh.at[0], h_ss.at[1], h_rs.at[0], prv),
    ]
    for cp in halo:
        cp.start()
    swap = [
        rcopy(tin_h, tin_k, t_ss.at[0], t_rs.at[0], sib),
        rcopy(tout_h, tout_k, t_ss.at[1], t_rs.at[1], sib),
    ]
    for cp in swap:
        cp.start()

    def bias_src(b, ch, core):
        return zb.at[8 * b + ch, core]

    def bias_send(b, j, core):
        ch = (i + j) % NCH
        return rcopy(
            bias_src(b, ch, core), bb.at[b, c], b_ss.at[b, 2 * j + core], b_rs.at[b, c], (r, 2 * ch + core)
        )

    def bias_sib(b):
        return rcopy(bias_src(b, i, 1 - k), bb.at[b, c], b_ss.at[b, 0], b_rs.at[b, c], sib)

    b_sent = []

    def some_bulk(when):
        for b, j, core in BULK[when]:
            b_sent.append(bias_sib(b) if j == 0 else bias_send(b, j, core))
            b_sent[-1].start()

    bias_part(0, POST, sizes)
    some_bulk(0)
    for cp in ld_enc:
        cp.wait()
    for cp in halo:
        cp.wait_recv()
    rowi = iota((128, 256), 0)
    coli = iota((128, 256), 1)
    glob = flat * 128 + jnp.where(coli < 192, coli, coli - 256)
    start = jnp.where(
        rowi < 64, jnp.where(rowi < 32, ws[0], ws[1]), jnp.where(rowi < 96, ws[2], ws[3])
    )
    start = jnp.maximum(start, 0)
    stop = jnp.where(
        rowi < 64, jnp.where(rowi < 32, ws[0], ws[1]), jnp.where(rowi < 96, ws[2], ws[3])
    ) + 128
    stop = jnp.minimum(stop, NR * NC * 128)
    valid = jnp.logical_and(glob >= start, glob < stop)
    xf = jnp.concatenate([x_in[...], xh[0], xh[1]], 0).astype(F32)
    x1 = atom_layer(xf, valid, enc_in, enc_out)
    tokrow = (tok[...] - 192 * r).astype(F32)
    tokrows = jnp.broadcast_to(tokrow, (16, 128)).astype(BF16)
    x1all[c, 0:16, :] = tokrows
    x1all[c, 16:144, :] = x1
    x1all[c, 144:160, :] = tokrows

    edge = [
        rcopy(x1all.at[c, 80:160], xe.at[1], e_ss.at[0], e_rs.at[1], nxt),
        rcopy(x1all.at[c, 0:80], xe.at[0], e_ss.at[1], e_rs.at[0], prv),
    ]

    def x1_slot(s):
        return x1all.at[s, 0:144]

    x_send = [
        rcopy(x1_slot(c), x1_slot(c), x_ss.at[j], x_rs.at[c], chip(j)) for j in FAR_FIRST
    ]
    x_fwd = []
    for j in range(NCH):
        s = 2 * ((i + j) % NCH) + k
        x_fwd.append(rcopy(x1_slot(s), x1_slot(s), x_ss.at[NCH + j], x_rs.at[s], sib))
    x_far = []
    for j in range(NCH):
        s = 2 * ((i + j) % NCH) + 1 - k
        x_far.append(rcopy(x1_slot(s), x1_slot(s), x_ss.at[NCH + j], x_rs.at[s], sib))
    for cp in x_send:
        cp.start()
    x_fwd[0].start()
    for cp in edge:
        cp.start()

    ld_pair[2].wait()
    ld_pair[3].wait()
    bias_part(1, (0, 1, 2), no_sizes)
    b_own = []
    for b in range(2):
        cp = pltpu.make_async_copy(bias_src(b, i, k), bb.at[b, c], lsem.at[nload[0] + b])
        cp.start()
        b_own.append(cp)


    for cp in ld_slab:
        cp.wait()
    e_row = iota((256, 256), 0) - shift
    e_col = iota((256, 256), 1)

    def picker(lo, hi, first):
        hit = jnp.logical_and(e_col >= lo, e_col < hi)
        return jnp.logical_and(hit, e_row == e_col - lo + first)

    def onehot(m):
        return jnp.where(m, 1.0, 0.0).astype(BF16)

    pick_q = onehot(picker(0, 96, 0))
    pick_g = onehot(jnp.logical_or(picker(128, 192, 32), picker(224, 256, 0)))
    pick_k = onehot(picker(0, 96, 0))
    pick_v = onehot(picker(96, 192, 0))

    some_bulk(2)
    @pl.loop(0, 2)
    def _(m):
        wq[2 * m] = (dot(slab[4 * m], pick_q) + dot(slab[4 * m + 3], pick_g)).astype(BF16)
        wq[2 * m + 1] = (dot(slab[4 * m + 1], pick_k) + dot(slab[4 * m + 2], pick_v)).astype(BF16)

    for cp in ld_pool:
        cp.wait()
    want = (iota((QT, 128), 0) + QT * k).astype(F32)

    def pool_group(slots, first):
        xs = jnp.concatenate([x1all[s, 16:144, :] for s in slots], 0)
        feats = jnp.maximum(dot(xs, pool[...]), 0.0).astype(BF16)
        hots = []
        n = jnp.zeros((QT, 128), F32)
        for s in slots:
            t = x1all[s, 0:16, :].astype(F32)[0:1]
            hots.append(jnp.where(t == want, 1.0, 0.0))
            n = n + hots[-1]
        part = dot(jnp.concatenate(hots, 1).astype(BF16), feats)
        act[...] = part if first else act[...] + part
        return n

    near4, far4 = (0, 2, 6, 1), (7, 4, 3, 5)
    cnt = jnp.zeros((QT, 128), F32)
    for quad in (near4, far4):
        for j in quad:
            s = 2 * ((i + j) % NCH) + k
            if j > 0:
                rcopy(x1_slot(s), x1_slot(s), x_ss.at[0], x_rs.at[s], sib).wait_recv()
                x_fwd[j].start()
        cnt = cnt + pool_group([2 * ((i + j) % NCH) + k for j in quad], quad == near4)
    for quad in (near4, far4):
        for j in quad:
            x_far[j].wait_recv()
        cnt = cnt + pool_group([2 * ((i + j) % NCH) + 1 - k for j in quad], False)
    act[...] = act[...] / jnp.sum(cnt, -1, keepdims=True) + cond[...].astype(F32)

    nvalid = jnp.sum(
        jnp.sum(mask[...].astype(F32), 1, keepdims=True), 0, keepdims=True
    )
    lane = iota((1, 128), 1)
    lanef = lane.astype(F32)
    mine = 2 * r + k

    left = jnp.where(lane < 64, 1.0, 0.0).astype(BF16)
    right = jnp.where(lane < 64, 0.0, 1.0).astype(BF16)
    pad = jnp.zeros((32, 128), BF16)
    lq = iota((QT, 128), 1)

    def kv_slot(b, s):
        return kv.at[b, s]

    pend = []
    for b in range(2):
        n = normed(act[...]).astype(BF16)
        own_kv = dot(n, wq[2 * b + 1])
        kv[b, mine, 0] = own_kv[0:48, 0:128].astype(BF16)
        kv[b, mine, 1] = jnp.where(
            lane < 64, own_kv[0:48, 128:256], pltpu.roll(own_kv[48:96, 128:256], 64, 1)
        ).astype(BF16)
        kv[b, mine, 2] = own_kv[48:96, 0:128].astype(BF16)
        for j in FAR_FIRST:
            cp = rcopy(
                kv_slot(b, mine),
                kv_slot(b, mine),
                kv_ss.at[b, j],
                kv_rs.at[b, mine],
                ((r + j) % NR, c),
            )
            cp.start()
            pend.append(cp)
        fwd = []
        for j in range(NR):
            s = 2 * ((r + j) % NR) + k
            fwd.append(
                rcopy(kv_slot(b, s), kv_slot(b, s), kv_ss.at[b, NR + j], kv_rs.at[b, s], sib)
            )
        fwd[0].start()
        pend += fwd
        some_bulk(3 if b == 0 else 8)
        qg = dot(n, wq[2 * b])
        q = qg[:, 0:128].astype(BF16).astype(F32)
        gate = jax.nn.sigmoid(qg[:, 128:256])
        qs = jnp.concatenate([jnp.where(lq < 48, q, 0.0), jnp.where(lq < 48, 0.0, q)], 0).astype(
            BF16
        )
        for j in reversed(FAR_FIRST):
            s = 2 * ((r + j) % NR) + k
            rcopy(kv_slot(b, s), kv_slot(b, s), kv_ss.at[b, 0], kv_rs.at[b, s], sib).wait_recv()
            fwd[j].start()
        b_own[b].wait()
        for j in range(1, NC):
            s = (c + j) % NC
            rcopy(bb.at[b, s], bb.at[b, s], b_ss.at[b, 0], b_rs.at[b, s], sib).wait_recv()

        sizes = jnp.concatenate([bb[b, s, 72:ZR, :] for s in range(NC)], 0).astype(F32)
        steps = jnp.transpose(sizes * (1.0 / (32767.0 * 65536.0)))

        def scores(slots, steps, mx):
            keys = []
            for s in slots:
                keys += [kv[b, s, 0], kv[b, s, 2], pad]
            dots = dot_t(qs, jnp.concatenate(keys, 0)) * (1.0 / math.sqrt(48.0))
            for d, slot in enumerate(slots):
                first = (QT * slot).astype(F32)
                ok = lanef + first < jnp.minimum(nvalid, first + QT)
                word = bb[b, slot, 0:72, :]
                both = (lax.shift_right_logical(word, 16), word & 65535)
                parts = []
                for h in range(2):
                    step = steps[:, 8 * d + h : 8 * d + h + 1]
                    m = (both[h].astype(F32) - 32768.0) * step
                    tail = jnp.where(
                        lane < 32,
                        pltpu.roll(m[0:24], 32, 1),
                        jnp.where(
                            lane < 64, pltpu.roll(m[24:48], 64, 1), pltpu.roll(m[48:72], 96, 1)
                        ),
                    )
                    parts += [m, tail]
                sc = dots[:, 128 * d : 128 * d + 128] + jnp.concatenate(parts, 0)
                sc = jnp.where(ok, sc, NEG)
                ssc[slot] = sc
                mid = kv[b, slot, 1]
                vb[slot, 0:48, 0:128] = kv[b, slot, 0]
                vb[slot, 0:48, 128:256] = mid * left
                vb[slot, 48:96, 0:128] = kv[b, slot, 2]
                vb[slot, 48:96, 128:256] = mid * right
                mx = jnp.maximum(mx, sc)
            return mx

        mx = jnp.full((2 * QT, 128), 2 * NEG, F32)
        if b == 0:
            some_bulk(4)
        for turn in (0, 1, 3, 2):
            z = (r // 2 + turn) % 4
            for row in (2 * z, 2 * z + 1):
                s = 2 * row + 1 - k
                rcopy(kv_slot(b, s), kv_slot(b, s), kv_ss.at[b, 0], kv_rs.at[b, s], sib).wait_recv()
            slots = [4 * z + d for d in range(4)]
            near_steps = pltpu.roll(steps[0:72], (128 - 32 * z) % 128, 1)
            mx = scores(slots, near_steps, mx)
        top = jnp.max(mx, -1, keepdims=True)
        tot = jnp.zeros((2 * QT, 128), F32)
        ps = []
        for s in range(NC):
            e = jnp.exp(ssc[s] - top)
            tot = tot + e
            ps.append(e.astype(BF16))
        o = dot(jnp.concatenate(ps, 1), vb[...].reshape(NC * 128, 256))
        inv = 1.0 / jnp.sum(tot, -1, keepdims=True)
        o_a = o[:QT, 0:128] * inv[:QT]
        o_b = (o[:, 128:256] + pltpu.roll(o[:, 128:256], 64, 1)) * inv
        o = jnp.where(lq < 16, o_b[:QT], jnp.where(lq < 64, o_b[QT:], jnp.where(lq < 96, 0.0, o_a)))
        ob[b, i] = (gate * o).astype(BF16)
        for j in FAR_FIRST:
            cp = rcopy(ob.at[b, i], ob.at[b, i], o_ss.at[b, j], o_rs.at[b, i], chip(j))
            cp.start()
            pend.append(cp)
        if b == 0:
            some_bulk(5)
            for cp in ld_tok:
                cp.wait()
            for cp in swap:
                cp.wait_recv()
        for j in range(1, NCH):
            s = (i + j) % NCH
            rcopy(ob.at[b, s], ob.at[b, s], o_ss.at[b, 0], o_rs.at[b, s], sib).wait_recv()
        gated = jnp.concatenate([ob[b, s] for s in range(NCH)], 1)
        mid_act = act[...] + dot(gated, topad[8 * b : 8 * b + 8].reshape(1024, 768))
        act[...] = mid_act

        m = normed(mid_act).astype(BF16)
        swish = jax.nn.silu(dot_t(m, tin[b, 0]))
        hidden = (swish * dot_t(m, tin[b, 1])).astype(BF16)
        prt[b] = dot(hidden, tout[b]).astype(BF16)
        for u in range(OWN):

            @pl.when(unit != u)
            def _():
                rcopy(
                    prt.at[b, 16 * u : 16 * u + 16],
                    rsb.at[b, i],
                    r_ss.at[b, u],
                    r_rs.at[b, i],
                    owner_dev(u),
                ).start()

        if b == 0:
            some_bulk(6)

        @pl.when(is_owner)
        def _():
            row0 = pl.multiple_of(16 * unit, 16)
            rsb[b, i] = prt[b, pl.ds(row0, 16), :]
            for j in range(1, NCH):
                s = (i + j) % NCH
                rcopy(rsb.at[b, s], rsb.at[b, s], r_ss.at[b, 0], r_rs.at[b, s], sib).wait_recv()
            total = rsb[b, 0].astype(F32)
            for s in range(1, NCH):
                total = total + rsb[b, s].astype(F32)
            if b == 0:
                db[unit] = total.astype(BF16)
                for j in FAR_FIRST:
                    rcopy(
                        db.at[unit], db.at[unit], d_ss.at[j], d_rs.at[unit], chip(j)
                    ).start()
            else:
                last = act[pl.ds(row0, 16), :] + total
                here = pl.multiple_of(64 + QT * k + 16 * unit, 16)
                mine_p = proj.at[pl.ds(here, 16)]
                proj[pl.ds(here, 16), :] = dot(
                    normed(last).astype(BF16), tok_atom[...]
                ).astype(BF16)
                for j in range(1, NC):
                    rcopy(
                        mine_p, mine_p, p_ss.at[j], p_rs.at[OWN * k + unit], (r, (c + j) % NC)
                    ).start()

                @pl.when(is_tail)
                def _():
                    rcopy(
                        mine_p,
                        proj.at[pl.ds(pl.multiple_of(16 * (unit - 2), 16), 16)],
                        p_ss.at[16],
                        p_rs.at[10 + unit],
                        ((r + 1) % NR, 0),
                    ).start()

                @pl.when(is_head)
                def _():
                    rcopy(
                        mine_p,
                        proj.at[pl.ds(pl.multiple_of(256 + 16 * unit, 16), 16)],
                        p_ss.at[16],
                        p_rs.at[12 + unit],
                        ((r + NR - 1) % NR, NC - 1),
                    ).start()

        if b == 0:
            some_bulk(7)
            for o_ in range(OWN):

                @pl.when(unit != o_)
                def _():
                    rcopy(db.at[o_], db.at[o_], d_ss.at[0], d_rs.at[o_], sib).wait_recv()

            act[...] += jnp.concatenate([db[s].astype(F32) for s in range(OWN)], 0)

    for cp in edge:
        cp.wait_recv()
    half = iota((1, 128), 1) < 64
    high = xe[0, 0:16, :].astype(F32)[0:1] + jnp.where(c == NC - 1, 192.0, 0.0)
    low = xe[1, 64:80, :].astype(F32)[0:1] - jnp.where(c == 0, 192.0, 0.0)
    side = jnp.where(half, high, low) + 64.0
    tcol = jnp.concatenate(
        [
            jnp.transpose(jnp.broadcast_to(tokrow + 64.0, (128, 128))),
            jnp.transpose(jnp.broadcast_to(side, (128, 128))),
        ],
        0,
    )
    lane2 = iota((256, 128), 1).astype(F32)
    hot = jnp.concatenate(
        [jnp.where(tcol == lane2 + 128.0 * t, 1.0, 0.0) for t in range(3)], 1
    ).astype(BF16)
    x1cat = jnp.concatenate([x1all[c, 16:144, :], xe[0, 16:80, :], xe[1, 0:64, :]], 0).astype(F32)

    def proj_wait(slot, row, n):
        ref = proj.at[row : row + n]
        rcopy(ref, ref, p_ss.at[0], p_rs.at[slot], sib).wait_recv()

    for s in range(2 * OWN):

        @pl.when(jnp.logical_or(jnp.logical_not(is_owner), s != OWN * k + unit))
        def _():
            proj_wait(s, 64 + 16 * s, 16)

    @pl.when(c == 0)
    def _():
        for s in range(4):
            proj_wait(12 + s, 16 * s, 16)

    @pl.when(c == NC - 1)
    def _():
        for s in range(4):
            proj_wait(12 + s, 256 + 16 * s, 16)

    spread = dot(hot, proj[...])
    x2 = (x1cat + spread).astype(BF16).astype(F32)
    x3 = atom_layer(x2, valid, dec_in, dec_out)
    n3 = normed(x3.astype(F32)).astype(BF16)
    out[...] = dot_t(pos[...], n3)

    for cp in halo + swap + edge + x_send + x_fwd + b_sent + pend:
        cp.wait_send()
    for b in range(2):
        for o_ in range(OWN):

            @pl.when(unit != o_)
            def _():
                src = prt.at[b, 16 * o_ : 16 * o_ + 16]
                rcopy(src, rsb.at[b, i], r_ss.at[b, o_], r_rs.at[b, i], sib).wait_send()

    @pl.when(is_owner)
    def _():
        for j in range(1, NCH):
            rcopy(db.at[0], db.at[0], d_ss.at[j], d_rs.at[0], sib).wait_send()
        ref = proj.at[pl.ds(pl.multiple_of(64 + QT * k + 16 * unit, 16), 16)]
        for j in range(1, NC):
            rcopy(ref, ref, p_ss.at[j], p_rs.at[0], sib).wait_send()

        @pl.when(jnp.logical_or(is_tail, is_head))
        def _():
            rcopy(ref, ref, p_ss.at[16], p_rs.at[0], sib).wait_send()


def body(
    atom_feat,
    atom_token,
    window_start,
    token_cond,
    token_mask,
    pair,
    enc_in,
    enc_out,
    pool_weight,
    tok_in,
    tok_out,
    pair_weight,
    trans_in,
    trans_out,
    tok_atom,
    dec_in,
    dec_out,
    pos_out,
):
    vm = pl.BlockSpec(memory_space=pltpu.VMEM)
    hb = pl.BlockSpec(memory_space=pl.ANY)
    dma = pltpu.SemaphoreType.DMA
    wt = jnp.transpose(pair_weight, (0, 2, 1)).reshape(32, 128)
    V = pltpu.VMEM
    scratch = [
        V((QT, 768), BF16),
        V((192, 96, 128), BF16),
        V((4, 128, 128), BF16),
        V((128, 128), BF16),
        V((128, 768), BF16),
        V((8, 768, 256), BF16),
        V((4, 768, 256), BF16),
        V((16, 128, 768), BF16),
        V((2, 2, 192, 768), BF16),
        V((2, 192, 768), BF16),
        V((768, 128), BF16),
        V((4, 128, 128), BF16),
        V((128, 128), BF16),
        V((3, 128), BF16),
        V((2, 64, 128), BF16),
        V((16, 160, 128), BF16),
        V((2, 80, 128), BF16),
        V((16, 2, ZR, 128), jnp.int32),
        V((2, 16, ZR, 128), jnp.int32),
        V((2, 16, 3, 48, 128), BF16),
        V((16, 192, 128), F32),
        V((16, 128, 256), BF16),
        V((2, 8, QT, 128), BF16),
        V((2, QT, 768), BF16),
        V((2, 8, 16, 768), BF16),
        V((6, 16, 768), BF16),
        V((QT, 768), F32),
        V((384, 128), BF16),
        dma((24,)),
        dma((2,)),
        dma((2,)),
        dma((16,)),
        dma((16,)),
        dma((2,)),
        dma((2,)),
        dma((2,)),
        dma((2,)),
        dma((2, 16)),
        dma((2, 16)),
        dma((2, 16)),
        dma((2, 16)),
        dma((2, 8)),
        dma((2, 8)),
        dma((2, 8)),
        dma((2, 8)),
        dma((8,)),
        dma((8,)),
        dma((17,)),
        dma((16,)),
    ]
    return pl.pallas_call(
        kernel,
        out_shape=jax.ShapeDtypeStruct((3, 128), F32),
        in_specs=[pl.BlockSpec(memory_space=pltpu.SMEM)] + [vm] * 4 + [hb] * 13,
        out_specs=vm,
        scratch_shapes=scratch,
        compiler_params=pltpu.CompilerParams(
            collective_id=0, has_side_effects=True, vmem_limit_bytes=56 << 20
        ),
        name="diffusion_step",
    )(
        window_start,
        atom_token.reshape(1, 128),
        token_mask.reshape(12, 128),
        atom_feat,
        wt,
        token_cond,
        pair,
        enc_in,
        enc_out,
        pool_weight,
        tok_in.reshape(8, 768, 768),
        tok_out.reshape(16, 96, 768),
        jnp.swapaxes(trans_in, 2, 3),
        trans_out,
        tok_atom,
        dec_in,
        dec_out,
        pos_out,
    )


def solution(mesh):
    in_specs = (
        P(("row", "col"), None),
        P(("row", "col")),
        P(("row", "col")),
        P("row", None),
        P(),
        P("row", "col", None),
        P(),
        P(),
        P(),
        P(),
        P(),
        P(),
        P(None, None, None, "col"),
        P(None, "col", None),
        P(),
        P(),
        P(),
        P(),
    )
    out_specs = P(None, ("row", "col"))
    return jax.shard_map(body, mesh=mesh, in_specs=in_specs, out_specs=out_specs, check_vma=False)
```

```python
import math

import jax
import jax.numpy as jnp
from jax import lax
from jax.experimental import pallas as pl
from jax.experimental.pallas import tpu as pltpu
from jax.sharding import PartitionSpec as P

MESH = pl.DeviceIdType.MESH
F32 = jnp.float32
BF16 = jnp.bfloat16
NEG = -1000000000.0
NR = 8
NC = 16
NCH = 8
FAR_FIRST = (5, 3, 4, 1, 7, 2, 6)
OWN = 6
CHIP_OF = (0, 3, 6, 5, 2, 1)
QT = 96
BULK = (
    ((0, 2, 0), (0, 6, 0), (0, 4, 0), (0, 1, 0), (0, 7, 0), (0, 3, 0), (0, 5, 0)),
    (),
    ((0, 2, 1), (0, 6, 1), (0, 4, 1), (0, 1, 1), (0, 7, 1), (0, 3, 1), (0, 5, 1), (0, 0, 0)),
    ((1, 2, 0), (1, 6, 0), (1, 4, 0)),
    ((1, 2, 1), (1, 6, 1), (1, 4, 1), (1, 1, 0), (1, 1, 1)),
    ((1, 7, 0), (1, 7, 1)),
    ((1, 3, 0), (1, 3, 1)),
    ((1, 5, 0), (1, 5, 1), (1, 0, 0)),
    (),
)
PRE, POST = (0, 1), (2,)
ZR = 80
BT = 8


def dot(a, b):
    return jnp.dot(a, b, preferred_element_type=F32)


def dot_t(a, b):
    return lax.dot_general(a, b, (((1,), (1,)), ((), ())), preferred_element_type=F32)


def normed(x):
    cent = x - jnp.mean(x, -1, keepdims=True)
    var = jnp.mean(cent * cent, -1, keepdims=True)
    return cent * lax.rsqrt(var + 1e-05)


def iota(shape, dim):
    return lax.broadcasted_iota(jnp.int32, shape, dim)


def atom_layer(xf, valid, w_in, w_out):
    n = normed(xf).astype(BF16)
    own = n[:128]
    q = dot(own, w_in[0]).astype(BF16).astype(F32)
    keys = dot(n, w_in[1]).astype(BF16)
    vals = dot(n, w_in[2]).astype(BF16)
    gate = dot(own, w_in[3])
    head = iota((128, 128), 1) // 32
    outs = jnp.zeros((128, 128), F32)
    for h in range(4):
        qh = jnp.where(head == h, q, 0.0).astype(BF16)
        s = dot_t(qh, keys) * (1.0 / math.sqrt(32.0))
        s = jnp.where(valid, s, NEG)
        e = jnp.exp(s - jnp.max(s, -1, keepdims=True))
        total = jnp.sum(e, -1, keepdims=True)
        o = dot(e.astype(BF16), vals) / total
        outs = jnp.where(head == h, o, outs)
    gated = (jax.nn.sigmoid(gate) * outs).astype(BF16)
    return (xf[:128] + dot(gated, w_out[...])).astype(BF16)


def kernel(
    ws,
    tok,
    mask,
    x_in,
    wt,
    cond_h,
    pair_h,
    enc_in_h,
    enc_out_h,
    pool_h,
    tok_in_h,
    tok_out_h,
    tin_h,
    tout_h,
    tok_atom_h,
    dec_in_h,
    dec_out_h,
    pos_h,
    out,
    cond,
    pair,
    enc_in,
    enc_out,
    pool,
    slab,
    wq,
    topad,
    tin,
    tout,
    tok_atom,
    dec_in,
    dec_out,
    pos,
    xh,
    x1all,
    xe,
    zb,
    bb,
    kv,
    ssc,
    vb,
    ob,
    prt,
    rsb,
    db,
    act,
    proj,
    lsem,
    h_ss,
    h_rs,
    x_ss,
    x_rs,
    e_ss,
    e_rs,
    t_ss,
    t_rs,
    b_ss,
    b_rs,
    kv_ss,
    kv_rs,
    o_ss,
    o_rs,
    r_ss,
    r_rs,
    d_ss,
    d_rs,
    p_ss,
    p_rs,
):
    r = lax.axis_index("row")
    c = lax.axis_index("col")
    i = c // 2
    k = c % 2
    sib = (r, c + 1 - 2 * k)
    flat = r * NC + c
    nxt = (flat + 1) % (NR * NC)
    prv = (flat + NR * NC - 1) % (NR * NC)
    nxt = (nxt // NC, nxt % NC)
    prv = (prv // NC, prv % NC)
    turned = (i + 4 * k) % NCH
    unit = OWN + 0 * i
    for u in range(OWN):
        unit = jnp.where(turned == CHIP_OF[u], u, unit)
    is_owner = unit < OWN
    is_tail = jnp.logical_and(k == 1, jnp.logical_and(unit >= 2, is_owner))
    is_head = jnp.logical_and(k == 0, unit < 4)

    def owner_dev(u):
        return (r, 2 * ((CHIP_OF[u] + 4 * k) % NCH) + k)


    def chip(j):
        return (r, 2 * ((i + j) % NCH) + k)

    def rcopy(src, dst, ss, rs, dev):
        return pltpu.make_async_remote_copy(
            src_ref=src, dst_ref=dst, send_sem=ss, recv_sem=rs, device_id=dev, device_id_type=MESH
        )

    proj[...] = jnp.zeros((384, 128), BF16)

    bar = pltpu.get_barrier_semaphore()

    def greet(dev):
        pl.semaphore_signal(bar, inc=1, device_id=dev, device_id_type=MESH)

    for j in range(1, NC):
        greet((r, (c + j) % NC))
    for j in range(1, NR):
        greet(((r + j) % NR, c))
    greet(nxt)
    greet(prv)

    @pl.when(c == 0)
    def _():
        for u in range(2, OWN):
            greet(((r + NR - 1) % NR, 2 * ((CHIP_OF[u] + 4) % NCH) + 1))

    @pl.when(c == NC - 1)
    def _():
        for u in range(4):
            greet(((r + 1) % NR, 2 * CHIP_OF[u]))

    nload = [0]

    def load(src, dst):
        cp = pltpu.make_async_copy(src, dst, lsem.at[nload[0]])
        nload[0] += 1
        cp.start()
        return cp

    ld_pair = [load(pair_h.at[48 * j : 48 * j + 48], pair.at[48 * j : 48 * j + 48]) for j in range(4)]
    ld_enc = [load(enc_in_h, enc_in), load(enc_out_h, enc_out)]
    ld_pool = [
        load(pool_h, pool),
        load(cond_h.at[pl.ds(pl.multiple_of(QT * k, 32), QT)], cond),
    ]
    base = jnp.minimum(128 * ((QT * i) // 128), 512)
    base = pl.multiple_of(base, 128)
    shift = QT * i - base
    ld_slab = [load(tok_in_h.at[:, :, pl.ds(base, 256)], slab)]
    core_rows = pl.ds(pl.multiple_of(QT * k, 32), QT)
    tin_k = tin.at[:, :, core_rows, :]
    tout_k = tout.at[:, core_rows, :]
    ld_tok = [
        load(tok_out_h.at[:, 32:96], topad.at[:, 0:64]),
        load(tok_out_h.at[:, 0:32], topad.at[:, 96:128]),
        load(tin_h, tin_k),
        load(tout_h, tout_k),
        load(tok_atom_h, tok_atom),
        load(dec_in_h, dec_in),
        load(dec_out_h, dec_out),
        load(pos_h, pos),
    ]

    zb[:, :, 72:, :] = jnp.zeros((16, 2, 8, 128), jnp.int32)
    vb[:, 96:128, :] = jnp.zeros((16, 32, 256), BF16)
    topad[:, 64:96, :] = jnp.zeros((16, 32, 768), BF16)

    order = iota((32, 32), 1) == 16 * (iota((32, 32), 0) // 16) + 2 * (iota((32, 32), 0) % 8) + (
        iota((32, 32), 0) // 8
    ) % 2
    w_heads = dot(jnp.where(order, 1.0, 0.0).astype(BF16), wt[...]).astype(BF16)
    lane32 = iota((32, 128), 1)
    zf = zb.reshape(16 * 2 * ZR, 128)

    def bias_part(kp, parts, sizes):
        def words(u, first):
            return lax.shift_left(u[first : first + 8], 16) | u[first + 8 : first + 16]

        def put(b, row, value):
            zf[pl.ds(b * 16 * ZR + kp * ZR + row, 8, stride=2 * ZR), :] = value

        for kb in parts:

            def tiles(n, sizes):
                t = 24 * kb + BT * n
                rows = []
                for d in range(BT):
                    rows.append(pair[QT * kp + t + d])
                    rows.append(pair[QT * kp + 72 + BT * n + d, 32 * kb : 32 * kb + 32, :])
                res = dot_t(w_heads, jnp.concatenate(rows, 0))
                for d in range(BT):
                    x = res[:, 128 * d : 128 * d + 128]
                    most = jnp.max(jnp.abs(x), -1, keepdims=True)
                    size = (most * (65536.0 * 1.000001)).astype(jnp.int32) + 1
                    sizes = sizes + jnp.where(lane32 == t + d, size, 0)
                    inv = (32767.0 * 65536.0) / size.astype(F32)
                    u = (x * inv + 32768.5).astype(jnp.int32)
                    for b in range(2):
                        put(b, t + d, words(u, 16 * b))
                return sizes

            sizes = lax.fori_loop(0, 24 // BT, tiles, sizes)
        if 2 not in parts:
            return sizes
        for b in range(2):
            for odd in range(2):
                put(b, 72 + odd, sizes[16 * b + 8 * odd : 16 * b + 8 * odd + 8])

    ld_pair[0].wait()
    ld_pair[1].wait()
    no_sizes = jnp.zeros((32, 128), jnp.int32)
    sizes = bias_part(0, PRE, no_sizes)
    extra = jnp.where(jnp.logical_or(is_tail, is_head), 1, 0)
    pl.semaphore_wait(bar, 24 + extra)

    halo = [
        rcopy(x_in.at[64:128], xh.at[1], h_ss.at[0], h_rs.at[1], nxt),
        rcopy(x_in.at[0:64], xh.at[0], h_ss.at[1], h_rs.at[0], prv),
    ]
    for cp in halo:
        cp.start()
    swap = [
        rcopy(tin_h, tin_k, t_ss.at[0], t_rs.at[0], sib),
        rcopy(tout_h, tout_k, t_ss.at[1], t_rs.at[1], sib),
    ]
    for cp in swap:
        cp.start()

    def bias_src(b, ch, core):
        return zb.at[8 * b + ch, core]

    def bias_send(b, j, core):
        ch = (i + j) % NCH
        return rcopy(
            bias_src(b, ch, core), bb.at[b, c], b_ss.at[b, 2 * j + core], b_rs.at[b, c], (r, 2 * ch + core)
        )

    def bias_sib(b):
        return rcopy(bias_src(b, i, 1 - k), bb.at[b, c], b_ss.at[b, 0], b_rs.at[b, c], sib)

    b_sent = []

    def some_bulk(when):
        for b, j, core in BULK[when]:
            b_sent.append(bias_sib(b) if j == 0 else bias_send(b, j, core))
            b_sent[-1].start()

    bias_part(0, POST, sizes)
    some_bulk(0)
    for cp in ld_enc:
        cp.wait()
    for cp in halo:
        cp.wait_recv()
    rowi = iota((128, 256), 0)
    coli = iota((128, 256), 1)
    glob = flat * 128 + jnp.where(coli < 192, coli, coli - 256)
    start = jnp.where(
        rowi < 64, jnp.where(rowi < 32, ws[0], ws[1]), jnp.where(rowi < 96, ws[2], ws[3])
    )
    start = jnp.maximum(start, 0)
    stop = jnp.where(
        rowi < 64, jnp.where(rowi < 32, ws[0], ws[1]), jnp.where(rowi < 96, ws[2], ws[3])
    ) + 128
    stop = jnp.minimum(stop, NR * NC * 128)
    valid = jnp.logical_and(glob >= start, glob < stop)
    xf = jnp.concatenate([x_in[...], xh[0], xh[1]], 0).astype(F32)
    x1 = atom_layer(xf, valid, enc_in, enc_out)
    tokrow = (tok[...] - 192 * r).astype(F32)
    tokrows = jnp.broadcast_to(tokrow, (16, 128)).astype(BF16)
    x1all[c, 0:16, :] = tokrows
    x1all[c, 16:144, :] = x1
    x1all[c, 144:160, :] = tokrows

    edge = [
        rcopy(x1all.at[c, 80:160], xe.at[1], e_ss.at[0], e_rs.at[1], nxt),
        rcopy(x1all.at[c, 0:80], xe.at[0], e_ss.at[1], e_rs.at[0], prv),
    ]

    def x1_slot(s):
        return x1all.at[s, 0:144]

    x_send = [
        rcopy(x1_slot(c), x1_slot(c), x_ss.at[j], x_rs.at[c], chip(j)) for j in FAR_FIRST
    ]
    x_fwd = []
    for j in range(NCH):
        s = 2 * ((i + j) % NCH) + k
        x_fwd.append(rcopy(x1_slot(s), x1_slot(s), x_ss.at[NCH + j], x_rs.at[s], sib))
    x_far = []
    for j in range(NCH):
        s = 2 * ((i + j) % NCH) + 1 - k
        x_far.append(rcopy(x1_slot(s), x1_slot(s), x_ss.at[NCH + j], x_rs.at[s], sib))
    for cp in x_send:
        cp.start()
    x_fwd[0].start()
    for cp in edge:
        cp.start()

    ld_pair[2].wait()
    ld_pair[3].wait()
    bias_part(1, (0, 1, 2), no_sizes)
    b_own = []
    for b in range(2):
        cp = pltpu.make_async_copy(bias_src(b, i, k), bb.at[b, c], lsem.at[nload[0] + b])
        cp.start()
        b_own.append(cp)


    for cp in ld_slab:
        cp.wait()
    e_row = iota((256, 256), 0) - shift
    e_col = iota((256, 256), 1)

    def picker(lo, hi, first):
        hit = jnp.logical_and(e_col >= lo, e_col < hi)
        return jnp.logical_and(hit, e_row == e_col - lo + first)

    def onehot(m):
        return jnp.where(m, 1.0, 0.0).astype(BF16)

    pick_q = onehot(picker(0, 96, 0))
    pick_g = onehot(jnp.logical_or(picker(128, 192, 32), picker(224, 256, 0)))
    pick_k = onehot(picker(0, 96, 0))
    pick_v = onehot(picker(96, 192, 0))

    some_bulk(2)
    @pl.loop(0, 2)
    def _(m):
        wq[2 * m] = (dot(slab[4 * m], pick_q) + dot(slab[4 * m + 3], pick_g)).astype(BF16)
        wq[2 * m + 1] = (dot(slab[4 * m + 1], pick_k) + dot(slab[4 * m + 2], pick_v)).astype(BF16)

    for cp in ld_pool:
        cp.wait()
    want = (iota((QT, 128), 0) + QT * k).astype(F32)

    def pool_group(slots, first):
        xs = jnp.concatenate([x1all[s, 16:144, :] for s in slots], 0)
        feats = jnp.maximum(dot(xs, pool[...]), 0.0).astype(BF16)
        hots = []
        n = jnp.zeros((QT, 128), F32)
        for s in slots:
            t = x1all[s, 0:16, :].astype(F32)[0:1]
            hots.append(jnp.where(t == want, 1.0, 0.0))
            n = n + hots[-1]
        part = dot(jnp.concatenate(hots, 1).astype(BF16), feats)
        act[...] = part if first else act[...] + part
        return n

    near4, far4 = (0, 2, 6, 1), (7, 4, 3, 5)
    cnt = jnp.zeros((QT, 128), F32)
    for quad in (near4, far4):
        for j in quad:
            s = 2 * ((i + j) % NCH) + k
            if j > 0:
                rcopy(x1_slot(s), x1_slot(s), x_ss.at[0], x_rs.at[s], sib).wait_recv()
                x_fwd[j].start()
        cnt = cnt + pool_group([2 * ((i + j) % NCH) + k for j in quad], quad == near4)
    for quad in (near4, far4):
        for j in quad:
            x_far[j].wait_recv()
        cnt = cnt + pool_group([2 * ((i + j) % NCH) + 1 - k for j in quad], False)
    act[...] = act[...] / jnp.sum(cnt, -1, keepdims=True) + cond[...].astype(F32)

    nvalid = jnp.sum(
        jnp.sum(mask[...].astype(F32), 1, keepdims=True), 0, keepdims=True
    )
    lane = iota((1, 128), 1)
    lanef = lane.astype(F32)
    mine = 2 * r + k

    left = jnp.where(lane < 64, 1.0, 0.0).astype(BF16)
    right = jnp.where(lane < 64, 0.0, 1.0).astype(BF16)
    pad = jnp.zeros((32, 128), BF16)
    lq = iota((QT, 128), 1)

    def kv_slot(b, s):
        return kv.at[b, s]

    pend = []
    for b in range(2):
        n = normed(act[...]).astype(BF16)
        own_kv = dot(n, wq[2 * b + 1])
        kv[b, mine, 0] = own_kv[0:48, 0:128].astype(BF16)
        kv[b, mine, 1] = jnp.where(
            lane < 64, own_kv[0:48, 128:256], pltpu.roll(own_kv[48:96, 128:256], 64, 1)
        ).astype(BF16)
        kv[b, mine, 2] = own_kv[48:96, 0:128].astype(BF16)
        for j in FAR_FIRST:
            cp = rcopy(
                kv_slot(b, mine),
                kv_slot(b, mine),
                kv_ss.at[b, j],
                kv_rs.at[b, mine],
                ((r + j) % NR, c),
            )
            cp.start()
            pend.append(cp)
        fwd = []
        for j in range(NR):
            s = 2 * ((r + j) % NR) + k
            fwd.append(
                rcopy(kv_slot(b, s), kv_slot(b, s), kv_ss.at[b, NR + j], kv_rs.at[b, s], sib)
            )
        fwd[0].start()
        pend += fwd
        some_bulk(3 if b == 0 else 8)
        qg = dot(n, wq[2 * b])
        q = qg[:, 0:128].astype(BF16).astype(F32)
        gate = jax.nn.sigmoid(qg[:, 128:256])
        qs = jnp.concatenate([jnp.where(lq < 48, q, 0.0), jnp.where(lq < 48, 0.0, q)], 0).astype(
            BF16
        )
        for j in reversed(FAR_FIRST):
            s = 2 * ((r + j) % NR) + k
            rcopy(kv_slot(b, s), kv_slot(b, s), kv_ss.at[b, 0], kv_rs.at[b, s], sib).wait_recv()
            fwd[j].start()
        b_own[b].wait()
        for j in range(1, NC):
            s = (c + j) % NC
            rcopy(bb.at[b, s], bb.at[b, s], b_ss.at[b, 0], b_rs.at[b, s], sib).wait_recv()

        sizes = jnp.concatenate([bb[b, s, 72:ZR, :] for s in range(NC)], 0).astype(F32)
        steps = jnp.transpose(sizes * (1.0 / (32767.0 * 65536.0)))

        def scores(slots, steps, mx):
            keys = []
            for s in slots:
                keys += [kv[b, s, 0], kv[b, s, 2], pad]
            dots = dot_t(qs, jnp.concatenate(keys, 0)) * (1.0 / math.sqrt(48.0))
            for d, slot in enumerate(slots):
                first = (QT * slot).astype(F32)
                ok = lanef + first < jnp.minimum(nvalid, first + QT)
                word = bb[b, slot, 0:72, :]
                both = (lax.shift_right_logical(word, 16), word & 65535)
                parts = []
                for h in range(2):
                    step = steps[:, 8 * d + h : 8 * d + h + 1]
                    m = (both[h].astype(F32) - 32768.0) * step
                    tail = jnp.where(
                        lane < 32,
                        pltpu.roll(m[0:24], 32, 1),
                        jnp.where(
                            lane < 64, pltpu.roll(m[24:48], 64, 1), pltpu.roll(m[48:72], 96, 1)
                        ),
                    )
                    parts += [m, tail]
                sc = dots[:, 128 * d : 128 * d + 128] + jnp.concatenate(parts, 0)
                sc = jnp.where(ok, sc, NEG)
                ssc[slot] = sc
                mid = kv[b, slot, 1]
                vb[slot, 0:48, 0:128] = kv[b, slot, 0]
                vb[slot, 0:48, 128:256] = mid * left
                vb[slot, 48:96, 0:128] = kv[b, slot, 2]
                vb[slot, 48:96, 128:256] = mid * right
                mx = jnp.maximum(mx, sc)
            return mx

        mx = jnp.full((2 * QT, 128), 2 * NEG, F32)
        if b == 0:
            some_bulk(4)
        for turn in (0, 1, 3, 2):
            z = (r // 2 + turn) % 4
            for row in (2 * z, 2 * z + 1):
                s = 2 * row + 1 - k
                rcopy(kv_slot(b, s), kv_slot(b, s), kv_ss.at[b, 0], kv_rs.at[b, s], sib).wait_recv()
            slots = [4 * z + d for d in range(4)]
            near_steps = pltpu.roll(steps[0:72], (128 - 32 * z) % 128, 1)
            mx = scores(slots, near_steps, mx)
        top = jnp.max(mx, -1, keepdims=True)
        tot = jnp.zeros((2 * QT, 128), F32)
        ps = []
        for s in range(NC):
            e = jnp.exp(ssc[s] - top)
            tot = tot + e
            ps.append(e.astype(BF16))
        o = dot(jnp.concatenate(ps, 1), vb[...].reshape(NC * 128, 256))
        inv = 1.0 / jnp.sum(tot, -1, keepdims=True)
        o_a = o[:QT, 0:128] * inv[:QT]
        o_b = (o[:, 128:256] + pltpu.roll(o[:, 128:256], 64, 1)) * inv
        o = jnp.where(lq < 16, o_b[:QT], jnp.where(lq < 64, o_b[QT:], jnp.where(lq < 96, 0.0, o_a)))
        ob[b, i] = (gate * o).astype(BF16)
        for j in FAR_FIRST:
            cp = rcopy(ob.at[b, i], ob.at[b, i], o_ss.at[b, j], o_rs.at[b, i], chip(j))
            cp.start()
            pend.append(cp)
        if b == 0:
            some_bulk(5)
            for cp in ld_tok:
                cp.wait()
            for cp in swap:
                cp.wait_recv()
        mid_act = act[...]
        for quad in (near4, far4):
            gated = []
            weights = []
            for j in quad:
                s = (i + j) % NCH
                if j > 0:
                    rcopy(ob.at[b, s], ob.at[b, s], o_ss.at[b, 0], o_rs.at[b, s], sib).wait_recv()
                gated.append(ob[b, s])
                weights.append(topad[8 * b + s])
            mid_act = mid_act + dot(jnp.concatenate(gated, 1), jnp.concatenate(weights, 0))
        act[...] = mid_act

        m = normed(mid_act).astype(BF16)
        swish = jax.nn.silu(dot_t(m, tin[b, 0]))
        hidden = (swish * dot_t(m, tin[b, 1])).astype(BF16)
        prt[b] = dot(hidden, tout[b]).astype(BF16)
        for u in range(OWN):

            @pl.when(unit != u)
            def _():
                rcopy(
                    prt.at[b, 16 * u : 16 * u + 16],
                    rsb.at[b, i],
                    r_ss.at[b, u],
                    r_rs.at[b, i],
                    owner_dev(u),
                ).start()

        if b == 0:
            some_bulk(6)

        @pl.when(is_owner)
        def _():
            row0 = pl.multiple_of(16 * unit, 16)
            rsb[b, i] = prt[b, pl.ds(row0, 16), :]
            for j in range(1, NCH):
                s = (i + j) % NCH
                rcopy(rsb.at[b, s], rsb.at[b, s], r_ss.at[b, 0], r_rs.at[b, s], sib).wait_recv()
            total = rsb[b, 0].astype(F32)
            for s in range(1, NCH):
                total = total + rsb[b, s].astype(F32)
            if b == 0:
                db[unit] = total.astype(BF16)
                for j in FAR_FIRST:
                    rcopy(
                        db.at[unit], db.at[unit], d_ss.at[j], d_rs.at[unit], chip(j)
                    ).start()
            else:
                last = act[pl.ds(row0, 16), :] + total
                here = pl.multiple_of(64 + QT * k + 16 * unit, 16)
                mine_p = proj.at[pl.ds(here, 16)]
                proj[pl.ds(here, 16), :] = dot(
                    normed(last).astype(BF16), tok_atom[...]
                ).astype(BF16)
                for j in range(1, NC):
                    rcopy(
                        mine_p, mine_p, p_ss.at[j], p_rs.at[OWN * k + unit], (r, (c + j) % NC)
                    ).start()

                @pl.when(is_tail)
                def _():
                    rcopy(
                        mine_p,
                        proj.at[pl.ds(pl.multiple_of(16 * (unit - 2), 16), 16)],
                        p_ss.at[16],
                        p_rs.at[10 + unit],
                        ((r + 1) % NR, 0),
                    ).start()

                @pl.when(is_head)
                def _():
                    rcopy(
                        mine_p,
                        proj.at[pl.ds(pl.multiple_of(256 + 16 * unit, 16), 16)],
                        p_ss.at[16],
                        p_rs.at[12 + unit],
                        ((r + NR - 1) % NR, NC - 1),
                    ).start()

        if b == 0:
            some_bulk(7)
            for o_ in range(OWN):

                @pl.when(unit != o_)
                def _():
                    rcopy(db.at[o_], db.at[o_], d_ss.at[0], d_rs.at[o_], sib).wait_recv()

            act[...] += jnp.concatenate([db[s].astype(F32) for s in range(OWN)], 0)

    for cp in edge:
        cp.wait_recv()
    half = iota((1, 128), 1) < 64
    high = xe[0, 0:16, :].astype(F32)[0:1] + jnp.where(c == NC - 1, 192.0, 0.0)
    low = xe[1, 64:80, :].astype(F32)[0:1] - jnp.where(c == 0, 192.0, 0.0)
    side = jnp.where(half, high, low) + 64.0
    tcol = jnp.concatenate(
        [
            jnp.transpose(jnp.broadcast_to(tokrow + 64.0, (128, 128))),
            jnp.transpose(jnp.broadcast_to(side, (128, 128))),
        ],
        0,
    )
    lane2 = iota((256, 128), 1).astype(F32)
    hot = jnp.concatenate(
        [jnp.where(tcol == lane2 + 128.0 * t, 1.0, 0.0) for t in range(3)], 1
    ).astype(BF16)
    x1cat = jnp.concatenate([x1all[c, 16:144, :], xe[0, 16:80, :], xe[1, 0:64, :]], 0).astype(F32)

    def proj_wait(slot, row, n):
        ref = proj.at[row : row + n]
        rcopy(ref, ref, p_ss.at[0], p_rs.at[slot], sib).wait_recv()

    for cp in halo + swap + edge + x_send + x_fwd + b_sent + pend:
        cp.wait_send()
    for b in range(2):
        for o_ in range(OWN):

            @pl.when(unit != o_)
            def _():
                src = prt.at[b, 16 * o_ : 16 * o_ + 16]
                rcopy(src, rsb.at[b, i], r_ss.at[b, o_], r_rs.at[b, i], sib).wait_send()

    for s in range(2 * OWN):

        @pl.when(jnp.logical_or(jnp.logical_not(is_owner), s != OWN * k + unit))
        def _():
            proj_wait(s, 64 + 16 * s, 16)

    @pl.when(c == 0)
    def _():
        for s in range(4):
            proj_wait(12 + s, 16 * s, 16)

    @pl.when(c == NC - 1)
    def _():
        for s in range(4):
            proj_wait(12 + s, 256 + 16 * s, 16)

    spread = dot(hot, proj[...])
    x2 = (x1cat + spread).astype(BF16).astype(F32)
    x3 = atom_layer(x2, valid, dec_in, dec_out)
    n3 = normed(x3.astype(F32)).astype(BF16)
    out[...] = dot_t(pos[...], n3)

    @pl.when(is_owner)
    def _():
        for j in range(1, NCH):
            rcopy(db.at[0], db.at[0], d_ss.at[j], d_rs.at[0], sib).wait_send()
        ref = proj.at[pl.ds(pl.multiple_of(64 + QT * k + 16 * unit, 16), 16)]
        for j in range(1, NC):
            rcopy(ref, ref, p_ss.at[j], p_rs.at[0], sib).wait_send()

        @pl.when(jnp.logical_or(is_tail, is_head))
        def _():
            rcopy(ref, ref, p_ss.at[16], p_rs.at[0], sib).wait_send()


def body(
    atom_feat,
    atom_token,
    window_start,
    token_cond,
    token_mask,
    pair,
    enc_in,
    enc_out,
    pool_weight,
    tok_in,
    tok_out,
    pair_weight,
    trans_in,
    trans_out,
    tok_atom,
    dec_in,
    dec_out,
    pos_out,
):
    vm = pl.BlockSpec(memory_space=pltpu.VMEM)
    hb = pl.BlockSpec(memory_space=pl.ANY)
    dma = pltpu.SemaphoreType.DMA
    wt = jnp.transpose(pair_weight, (0, 2, 1)).reshape(32, 128)
    V = pltpu.VMEM
    scratch = [
        V((QT, 768), BF16),
        V((192, 96, 128), BF16),
        V((4, 128, 128), BF16),
        V((128, 128), BF16),
        V((128, 768), BF16),
        V((8, 768, 256), BF16),
        V((4, 768, 256), BF16),
        V((16, 128, 768), BF16),
        V((2, 2, 192, 768), BF16),
        V((2, 192, 768), BF16),
        V((768, 128), BF16),
        V((4, 128, 128), BF16),
        V((128, 128), BF16),
        V((3, 128), BF16),
        V((2, 64, 128), BF16),
        V((16, 160, 128), BF16),
        V((2, 80, 128), BF16),
        V((16, 2, ZR, 128), jnp.int32),
        V((2, 16, ZR, 128), jnp.int32),
        V((2, 16, 3, 48, 128), BF16),
        V((16, 192, 128), F32),
        V((16, 128, 256), BF16),
        V((2, 8, QT, 128), BF16),
        V((2, QT, 768), BF16),
        V((2, 8, 16, 768), BF16),
        V((6, 16, 768), BF16),
        V((QT, 768), F32),
        V((384, 128), BF16),
        dma((24,)),
        dma((2,)),
        dma((2,)),
        dma((16,)),
        dma((16,)),
        dma((2,)),
        dma((2,)),
        dma((2,)),
        dma((2,)),
        dma((2, 16)),
        dma((2, 16)),
        dma((2, 16)),
        dma((2, 16)),
        dma((2, 8)),
        dma((2, 8)),
        dma((2, 8)),
        dma((2, 8)),
        dma((8,)),
        dma((8,)),
        dma((17,)),
        dma((16,)),
    ]
    return pl.pallas_call(
        kernel,
        out_shape=jax.ShapeDtypeStruct((3, 128), F32),
        in_specs=[pl.BlockSpec(memory_space=pltpu.SMEM)] + [vm] * 4 + [hb] * 13,
        out_specs=vm,
        scratch_shapes=scratch,
        compiler_params=pltpu.CompilerParams(
            collective_id=0, has_side_effects=True, vmem_limit_bytes=56 << 20
        ),
        name="diffusion_step",
    )(
        window_start,
        atom_token.reshape(1, 128),
        token_mask.reshape(12, 128),
        atom_feat,
        wt,
        token_cond,
        pair,
        enc_in,
        enc_out,
        pool_weight,
        tok_in.reshape(8, 768, 768),
        tok_out.reshape(16, 96, 768),
        jnp.swapaxes(trans_in, 2, 3),
        trans_out,
        tok_atom,
        dec_in,
        dec_out,
        pos_out,
    )


def solution(mesh):
    in_specs = (
        P(("row", "col"), None),
        P(("row", "col")),
        P(("row", "col")),
        P("row", None),
        P(),
        P("row", "col", None),
        P(),
        P(),
        P(),
        P(),
        P(),
        P(),
        P(None, None, None, "col"),
        P(None, "col", None),
        P(),
        P(),
        P(),
        P(),
    )
    out_specs = P(None, ("row", "col"))
    return jax.shard_map(body, mesh=mesh, in_specs=in_specs, out_specs=out_specs, check_vma=False)
```
